128 devices in a mesh: dp: 8 (over x_lo, z), sky: 16 (over x_hi, y, core).
Axes of the slice: x: 4 (x_hi: 2, x_lo: 2; x = x_hi * 2 + x_lo), y: 4, z: 4, core: 2. Of those that a mesh axis runs over, the one named last changes fastest.
Arguments:
- queries: bfloat16 [8, 4096, 3072], P('dp', 'sky'), may hold values from -5 to 5
- key_states: bfloat16 [8, 4096, 3072], P('dp', 'sky'), may hold values from -5 to 5
- value_states: bfloat16 [8, 4096, 3072], P('dp', 'sky'), may hold values from -6 to 6
- key_blocks: int32 [16, 2], replicated, may hold values from -1 to 15, as said below
- global_block: int32 [1], replicated, may hold values from 0 to 15
- w_out: bfloat16 [3072, 3072], P('dp'), may hold values from -0.109375 to 0.109375
- grad_out: bfloat16 [8, 4096, 3072], P('dp', 'sky'), may hold values from -6 to 6
Outputs:
- attended: bfloat16 [8, 4096, 3072], P('dp', 'sky')
- grad_queries: bfloat16 [8, 4096, 3072], P('dp', 'sky')
- grad_keys: bfloat16 [8, 4096, 3072], P('dp', 'sky')
- grad_values: bfloat16 [8, 4096, 3072], P('dp', 'sky')
The draws below stay inside these ranges and needn't reach their ends.
Inputs may be any that keep to these rules, and one draw needn't show every extreme that they name: key_blocks[b, 0] is b - 1 or -1 and key_blocks[b, 1] is b + 1 or -1; -1 marks a missing neighbour. key_blocks[0, 0] and key_blocks[15, 1] are -1, key_blocks[14, 1] is 15.
All inputs are finite; a program needn't handle non-finite values.
Results may differ from the reference program's by a relative error of at most 0.03.
Values may be sent and summed in bfloat16 or wider, within the bound.
No kernel may reach another device: no remote copies, remote signals or barrier semaphores. Data moves between devices by JAX's collectives and lax.ppermute only.
A program may use at most 256 MiB of HBM per device.

```python
import math
import jax
import jax.numpy as jnp
from jax import lax

D = 3072
HEADS = 24
HD = 128
BLK = 256
HW = 3072
SAMPLES = 8
SEQ = 4096
NQB = 16


def draw_queries(key, part):
    key = jax.random.fold_in(key, 11)
    base = jnp.clip(jax.random.normal(key, (SAMPLES, SEQ, HW), jnp.float32), -5.0, 5.0)
    return base.astype(jnp.bfloat16)


def draw_key_states(key, part):
    key = jax.random.fold_in(key, 17)
    base = jnp.clip(jax.random.normal(key, (SAMPLES, SEQ, HW), jnp.float32), -5.0, 5.0)
    return base.astype(jnp.bfloat16)


def draw_key_blocks(key, part):
    key = jax.random.fold_in(key, 29)
    first_key, second_key = jax.random.split(key)
    index = jnp.arange(NQB, dtype=jnp.int32)
    keep_above = (jax.random.randint(first_key, (NQB,), 0, 4) > 0) & (index > 0)
    keep_below = ((jax.random.randint(second_key, (NQB,), 0, 4) > 0) | (index == NQB - 2)) & (index < NQB - 1)
    above_id = jnp.where(keep_above, index - 1, -1)
    below_id = jnp.where(keep_below, index + 1, -1)
    return jnp.stack([above_id, below_id], axis=1).astype(jnp.int32)


def levels(own_key, shape, shards, least, largest):
    loudness = 1.0
    for position, shards_of in shards:
        draws = jax.random.uniform(jax.random.fold_in(jax.random.fold_in(own_key, 6), position), (shards_of,), jnp.float32, least / len(shards), largest / len(shards))
        loudness = loudness * jnp.repeat(jnp.exp(draws), shape[position] // shards_of).reshape((-1,) + (1,) * (len(shape) - 1 - position))
    return loudness


def normal_values(own_key, shape, deviation, reach, cuts=(), kind=jnp.bfloat16):
    entries = jax.random.normal(own_key, shape, jnp.float32) * deviation
    if len(cuts) > 0:
        entries = levels(own_key, shape, cuts, -0.22, 0.18) * entries
    return jnp.clip(entries, min=-reach, max=reach).astype(kind)


def setup_inputs(seed: int = 0) -> dict:
    key_list = jax.random.split(jax.random.key(seed), 8)
    queries = draw_queries(jax.random.fold_in(key_list[7], 71), 0)
    key_states = draw_key_states(jax.random.fold_in(key_list[7], 71), 0)
    value_states = normal_values(key_list[2], (SAMPLES, SEQ, HW), 1.0, 6.0, ((0, 8), (1, 16)))
    key_blocks = draw_key_blocks(jax.random.fold_in(key_list[7], 71), 0)
    global_block = jax.random.randint(key_list[4], (1,), 0, NQB).astype(jnp.int32)
    w_out = normal_values(key_list[5], (HW, D), D ** -0.5, 0.109375, ((0, 8),))
    grad_out = normal_values(key_list[6], (SAMPLES, SEQ, D), 1.0, 6.0, ((0, 8), (1, 16)))
    return dict(queries=queries, key_states=key_states, value_states=value_states, key_blocks=key_blocks, global_block=global_block, w_out=w_out, grad_out=grad_out)


def block_attention(query, key_rows, value_rows, grad_attended, key_blocks, global_id):
    feature_width = query.shape[1]
    count = query.shape[0] // BLK
    score_scale = 1.0 / math.sqrt(HD)
    index = jnp.arange(count, dtype=jnp.int32)
    before = jnp.maximum(index - 1, 0).astype(jnp.int32)
    after = jnp.minimum(index + 1, count - 1).astype(jnp.int32)
    kv_blocks = jnp.stack([key_rows, value_rows]).reshape(2, count, BLK, feature_width)
    global_kv = lax.dynamic_index_in_dim(kv_blocks, global_id, 1, False)
    spread = jnp.broadcast_to(global_kv[:, None], kv_blocks.shape)
    slots = jnp.stack([kv_blocks, kv_blocks[:, before], kv_blocks[:, after], spread], axis=2)
    slots = slots.reshape(2, count, 4 * BLK, HEADS, HD).astype(jnp.float32)
    key_slots = slots[0]
    value_slots = slots[1]
    above_id = key_blocks[:, 0]
    below_id = key_blocks[:, 1]
    valid = jnp.stack([index >= 0, above_id >= 0, below_id >= 0, (global_id != index) & (global_id != above_id) & (global_id != below_id)], axis=1)
    keep = jnp.repeat(valid, BLK, axis=1)[:, None, None, :]
    query_rows = query.reshape(count, BLK, HEADS, HD).astype(jnp.float32)
    scores = jnp.einsum('jqhd,jkhd->jhqk', query_rows, key_slots) * score_scale
    scores = jnp.where(keep, scores, -jnp.inf)
    row_max = lax.optimization_barrier(jnp.max(scores, axis=-1, keepdims=True))
    exponent = jnp.exp(scores - row_max)
    attention = exponent / lax.optimization_barrier(jnp.sum(exponent, axis=-1, keepdims=True))
    attention_b = attention.astype(jnp.bfloat16).astype(jnp.float32)
    attended = jnp.einsum('jhqk,jkhd->jqhd', attention_b, value_slots).astype(jnp.bfloat16)
    grad_rows = grad_attended.reshape(count, BLK, HEADS, HD).astype(jnp.float32)
    delta = jnp.einsum('jqhd,jqhd->jhq', grad_rows, attended.astype(jnp.float32))
    grad_weights = jnp.einsum('jqhd,jkhd->jhqk', grad_rows, value_slots)
    grad_scores = (attention * (grad_weights - delta[..., None])).astype(jnp.bfloat16).astype(jnp.float32)
    grad_query = (jnp.einsum('jhqk,jkhd->jqhd', grad_scores, key_slots) * score_scale).astype(jnp.bfloat16)
    key_terms = jnp.einsum('jhqk,jqhd->jkhd', grad_scores, query_rows) * score_scale
    value_terms = jnp.einsum('jhqk,jqhd->jkhd', attention_b, grad_rows)
    terms = jnp.stack([key_terms, value_terms]).reshape(2, count, 4, BLK, feature_width)
    own_terms = terms[:, :, 0]
    up_terms = lax.optimization_barrier(terms[:, :, 1].astype(jnp.bfloat16)).astype(jnp.float32)
    down_terms = lax.optimization_barrier(terms[:, :, 2].astype(jnp.bfloat16)).astype(jnp.float32)
    global_sum = lax.optimization_barrier(jnp.sum(terms[:, :, 3], axis=1))
    empty = jnp.zeros_like(up_terms[:, :1])
    from_above = jnp.concatenate([up_terms[:, 1:], empty], axis=1)
    from_below = jnp.concatenate([empty, down_terms[:, :-1]], axis=1)
    hit = (index == global_id)[None, :, None, None]
    total = own_terms + from_above + from_below + jnp.where(hit, global_sum[:, None], jnp.float32(0.0))
    total = total.astype(jnp.bfloat16).reshape(2, count * BLK, feature_width)
    return (attended.reshape(count * BLK, feature_width), grad_query.reshape(count * BLK, feature_width), total[0], total[1])

def reference(queries, key_states, value_states, key_blocks, global_block, w_out, grad_out):
    grad_attended = jnp.einsum('std,hd->sth', grad_out.astype(jnp.float32), w_out.astype(jnp.float32)).astype(jnp.bfloat16)
    global_id = global_block[0].astype(jnp.int32)

    def one_sample(items):
        return block_attention(items[0], items[1], items[2], items[3], key_blocks, global_id)
    attended, grad_queries, grad_keys, grad_values = lax.map(one_sample, (queries, key_states, value_states, grad_attended))
    return (attended, grad_queries, grad_keys, grad_values)
```

```python
import functools
import math

import jax
import jax.numpy as jnp
from jax import lax
from jax.experimental import pallas as pl
from jax.experimental.pallas import tpu as pltpu
from jax.sharding import Mesh, PartitionSpec as P

HEADS = 24
HD = 128
BLK = 256
D = 3072
HALF = D // 2
PART = BLK // 4
PER = 3
SHARDS = 8
SCALE = 1.0 / math.sqrt(HD)
LOG2E = 1.4426950408889634
DP = ("x_lo", "z")
SKY = ("x_hi", "y", "core")
CHUNKS = ((0, 1), (1, 1), (2, 1))
F32 = jnp.float32
BF16 = jnp.bfloat16


def attention_kernel(info, q_ref, ko_ref, vo_ref, inner_ref, outer_ref, kg_ref, vg_ref, go_ref, wm_ref, wo_ref, *rest):
    att_ref, gq_ref, own_ref, tin_ref, tout_ref, keep_ref, send_ref = rest[-7:]
    core = info[3]
    across = (((1,), (1,)), ((), ()))
    q = q_ref[...]
    first = pl.multiple_of(core * HALF, HALF)
    second = pl.multiple_of((1 - core) * HALF, HALF)
    ga_t = lax.dot_general(wm_ref[...], go_ref[:, pl.ds(first, HALF)], across, preferred_element_type=F32)
    ga_t += lax.dot_general(wo_ref[...], go_ref[:, pl.ds(second, HALF)], across, preferred_element_type=F32)
    ga_tb = ga_t.astype(BF16)
    ga_r = ga_tb.astype(F32)
    ga = ga_r.T.astype(BF16)
    keys = [ko_ref[...], inner_ref[0], outer_ref[0], kg_ref[...]]
    values = [vo_ref[...], inner_ref[1], outer_ref[1], vg_ref[...]]
    scores = []
    for j in range(4):
        s = lax.dot_general(keys[j], q, across, preferred_element_type=F32) * (SCALE * LOG2E)
        if j > 0:
            s = s + jnp.where(info[j - 1] > 0, 0.0, -jnp.inf).astype(F32)
        scores.append(s)
    top = functools.reduce(jnp.maximum, [jnp.max(s, axis=0, keepdims=True) for s in scores])
    exps = [jnp.exp2(s - top) for s in scores]
    total = functools.reduce(jnp.add, [jnp.sum(e, axis=0, keepdims=True) for e in exps])
    inverse = 1.0 / total
    weights = [e * inverse for e in exps]
    weights_b = [p.astype(BF16) for p in weights]
    att_t = jnp.zeros((HD, BLK), F32)
    for j in range(4):
        att_t += jnp.dot(values[j].T, weights_b[j], preferred_element_type=F32)
    att_r = att_t.astype(BF16).astype(F32)
    att_ref[...] = att_r.T.astype(BF16)
    delta = jnp.sum(ga_r * att_r, axis=0, keepdims=True)
    gq_t = jnp.zeros((HD, BLK), F32)
    key_terms, value_terms = [], []
    for j in range(4):
        gw = jnp.dot(values[j], ga_tb, preferred_element_type=F32)
        gs = (weights[j] * (gw - delta)).astype(BF16)
        gq_t += jnp.dot(keys[j].T, gs, preferred_element_type=F32)
        key_terms.append((jnp.dot(gs, q, preferred_element_type=F32) * SCALE).astype(BF16))
        value_terms.append(jnp.dot(weights_b[j], ga, preferred_element_type=F32).astype(BF16))
    gq_ref[...] = (gq_t * SCALE).T.astype(BF16)
    for ref, j in ((own_ref, 0), (tin_ref, 1), (tout_ref, 2)):
        ref[0] = key_terms[j]
        ref[1] = value_terms[j]
    keep_ref[...] = jnp.where(core == 0, key_terms[3], value_terms[3])
    send_ref[...] = jnp.where(core == 0, value_terms[3], key_terms[3])


def attention(chunk, info, q, k, v, inner, outer, kg, vg, go, wm, wo, prior):
    start, n = chunk
    width = SHARDS * n * HD
    steps = SHARDS * n

    def head(t, *_):
        return (0, PER * (t // n) + start + t % n)

    def col(t, *_):
        return (0, t)

    def row(t, *_):
        return (t, 0)

    def pair(t, *_):
        return (0, 0, t)

    def whole(t, *_):
        return (0, 0)

    one = (BLK, HD)
    two = (2, BLK, HD)
    in_specs = [
        pl.BlockSpec(one, head),
        pl.BlockSpec(one, head),
        pl.BlockSpec(one, head),
        pl.BlockSpec(two, pair),
        pl.BlockSpec(two, pair),
        pl.BlockSpec(one, col),
        pl.BlockSpec(one, col),
        pl.BlockSpec((BLK, D), whole),
        pl.BlockSpec((HD, HALF), row),
        pl.BlockSpec((HD, HALF), row),
    ] + [pl.BlockSpec(memory_space=pl.ANY)] * len(prior)
    out_specs = [
        pl.BlockSpec(one, head),
        pl.BlockSpec(one, head),
        pl.BlockSpec(two, pair),
        pl.BlockSpec(two, pair),
        pl.BlockSpec(two, pair),
        pl.BlockSpec(one, col),
        pl.BlockSpec(one, col),
    ]
    full = jax.ShapeDtypeStruct((BLK, D), BF16)
    stacked = jax.ShapeDtypeStruct((2, BLK, width), BF16)
    single = jax.ShapeDtypeStruct((BLK, width), BF16)
    return pl.pallas_call(
        attention_kernel,
        grid_spec=pltpu.PrefetchScalarGridSpec(
            num_scalar_prefetch=1, grid=(steps,), in_specs=in_specs, out_specs=out_specs
        ),
        out_shape=[full, full, stacked, stacked, stacked, single, single],
        input_output_aliases={11: 0, 12: 1} if prior else {},
        compiler_params=pltpu.CompilerParams(vmem_limit_bytes=32 * 2**20),
        cost_estimate=pl.CostEstimate(
            flops=steps * (12 * BLK * 4 * BLK * HD + 2 * BLK * HD * D),
            bytes_accessed=steps * (BLK * HD * 2 * 20 + HD * D * 2),
            transcendentals=steps * BLK * 4 * BLK,
        ),
        name="attention",
    )(info, q, k, v, inner, outer, kg, vg, go, wm, wo, *prior)


def combine_kernel(info, own_ref, rin_ref, rout_ref, mine_ref, theirs_ref, *rest):
    gk_ref, gv_ref, total = rest[-3:]
    hit, y, core = info[4], info[5], info[3]
    total[...] = own_ref[...].astype(F32) + rin_ref[...].astype(F32) + rout_ref[...].astype(F32)

    @pl.when(hit > 0)
    def _():
        for r in range(4):
            place = pl.multiple_of(lax.rem(y + r, 4) * PART, PART)
            mine = mine_ref[r].astype(F32)
            theirs = theirs_ref[r].astype(F32)
            total[0, pl.ds(place, PART)] += jnp.where(core == 0, mine, theirs)
            total[1, pl.ds(place, PART)] += jnp.where(core == 0, theirs, mine)

    gk_ref[...] = total[0].astype(BF16)
    gv_ref[...] = total[1].astype(BF16)


def combine(chunk, info, own, rin, rout, mine, theirs, prior):
    start, n = chunk
    steps = SHARDS * n

    def head(t, *_):
        return (0, PER * (t // n) + start + t % n)

    def pair(t, *_):
        return (0, 0, t)

    two = pl.BlockSpec((2, BLK, HD), pair)
    quarters = pl.BlockSpec((4, PART, HD), pair)
    full = jax.ShapeDtypeStruct((BLK, D), BF16)
    return pl.pallas_call(
        combine_kernel,
        grid_spec=pltpu.PrefetchScalarGridSpec(
            num_scalar_prefetch=1,
            grid=(steps,),
            in_specs=[two, two, two, quarters, quarters] + [pl.BlockSpec(memory_space=pl.ANY)] * len(prior),
            out_specs=[pl.BlockSpec((BLK, HD), head)] * 2,
            scratch_shapes=[pltpu.VMEM((2, BLK, HD), F32)],
        ),
        out_shape=[full, full],
        input_output_aliases={6: 0, 7: 1} if prior else {},
        compiler_params=pltpu.CompilerParams(vmem_limit_bytes=32 * 2**20),
        cost_estimate=pl.CostEstimate(
            flops=steps * BLK * HD * 8, bytes_accessed=steps * BLK * HD * 2 * 12, transcendentals=0
        ),
        name="combine",
    )(info, own, rin, rout, mine, theirs, *prior)


def move(x, axis, step, size):
    return lax.ppermute(x, axis, [(i, (i + step) % size) for i in range(size)])


def swap_core(x):
    return move(x, "core", 1, 2)


def swap_outer(x):
    route = [(i, i + 1) for i in range(1, 15, 2)] + [(i + 1, i) for i in range(1, 15, 2)]
    return lax.ppermute(x, SKY, route)


def columns(x, chunk):
    start, n = chunk
    return x.reshape(BLK, SHARDS, PER, HD)[:, :, start : start + n].reshape(BLK, SHARDS * n * HD)


def spread_global(kv, inner, root, x, y, core):
    root_core, root_y, root_x = root % 2, (root // 2) % 4, root // 8
    source = jnp.where(root_core == core, kv, inner)
    cand = jnp.where(core == 0, source[0], source[1])
    pieces = [lax.dynamic_slice_in_dim(cand, ((y + r) % 4) * PART, PART, 0) for r in range(4)]
    arrived = [pieces[0]] + [move(pieces[r], "y", r, 4) for r in range(1, 4)]
    came = (y - root_y) % 4
    mine = arrived[0]
    for r in range(1, 4):
        mine = jnp.where(came == r, arrived[r], mine)
    other = move(mine, "x_hi", 1, 2)
    quarter = jnp.where(root_x == x, mine, other)
    parts = [quarter] + [move(quarter, "y", -r, 4) for r in range(1, 4)]
    held = jnp.concatenate(parts, axis=0)
    theirs = swap_core(held)
    return jnp.where(core == 0, held, theirs), jnp.where(core == 0, theirs, held)


def gather_terms(keep, send):
    both = (keep.astype(F32) + swap_core(send).astype(F32)).astype(BF16)
    arrived = [both[:PART]] + [move(both[r * PART : (r + 1) * PART], "y", r, 4) for r in range(1, 4)]
    quarter = functools.reduce(jnp.add, [a.astype(F32) for a in arrived]).astype(BF16)
    quarter = (quarter.astype(F32) + move(quarter, "x_hi", 1, 2).astype(F32)).astype(BF16)
    parts = [quarter] + [move(quarter, "y", -r, 4) for r in range(1, 4)]
    mine = jnp.stack(parts)
    return mine, swap_core(mine)


def local(queries, key_states, value_states, key_blocks, global_block, w_out, grad_out):
    x, y, core = lax.axis_index("x_hi"), lax.axis_index("y"), lax.axis_index("core")
    row = (x * 4 + y) * 2 + core
    root = global_block[0]
    ids = lax.dynamic_slice_in_dim(key_blocks, row, 1, 0)[0]
    above, below = ids[0], ids[1]
    inner_id = jnp.where(core == 0, below, above)
    outer_id = jnp.where(core == 0, above, below)
    live = (root != row) & (root != above) & (root != below)
    info = jnp.stack([inner_id >= 0, outer_id >= 0, live, core, root == row, y]).astype(jnp.int32)
    q, k, v, go = queries[0], key_states[0], value_states[0], grad_out[0]
    w_half = lax.dynamic_slice_in_dim(w_out, core * HALF, HALF, 1)
    grads, totals = (), ()
    for chunk in CHUNKS:
        start, n = chunk
        rows = w_half[start * HD : (start + n) * HD]
        wm = lax.all_gather(rows, DP, axis=0, tiled=True)
        wo = swap_core(wm)
        kv = jnp.stack([columns(k, chunk), columns(v, chunk)])
        inner = swap_core(kv)
        outer = swap_outer(kv)
        kg, vg = spread_global(kv, inner, root, x, y, core)
        out = attention(chunk, info, q, k, v, inner, outer, kg, vg, go, wm, wo, grads)
        grads = tuple(out[:2])
        own, tin, tout, keep, send = out[2:]
        rin, rout = swap_core(tin), swap_outer(tout)
        mine, theirs = gather_terms(keep, send)
        totals = tuple(combine(chunk, info, own, rin, rout, mine, theirs, totals))
    return tuple(a[None] for a in grads + totals)


def solution(mesh):
    inside = Mesh(mesh.devices.reshape(2, 4, 2, 4, 2), DP + SKY)
    rows = P(DP, SKY, None)
    return jax.shard_map(
        local,
        mesh=inside,
        in_specs=(rows, rows, rows, P(), P(), P(DP, None), rows),
        out_specs=(rows, rows, rows, rows),
        check_vma=False,
    )
```

```python
import functools
import math

import jax
import jax.numpy as jnp
from jax import lax
from jax.experimental import pallas as pl
from jax.experimental.pallas import tpu as pltpu
from jax.sharding import Mesh, PartitionSpec as P

HEADS = 24
HD = 128
BLK = 256
D = 3072
HALF = D // 2
PART = BLK // 4
ROWS = D // 8
PAIR = 2
SCALE = 1.0 / math.sqrt(HD)
LOG2E = 1.4426950408889634
DP = ("x_lo", "z")
SKY = ("x_hi", "y", "core")
CHUNK = 12
ACROSS = (((1,), (1,)), ((), ()))
F32 = jnp.float32
BF16 = jnp.bfloat16
VMEM = 60 * 2**20


ANY = pl.BlockSpec(memory_space=pl.ANY)


def project_kernel(mine_ref, theirs_ref, piece_ref, *rest):
    own_ref, send_ref = rest[-2:]
    piece = piece_ref[...]
    own_ref[...] = lax.dot_general(mine_ref[...], piece, ACROSS, preferred_element_type=F32)
    send_ref[...] = lax.dot_general(theirs_ref[...], piece, ACROSS, preferred_element_type=F32).astype(BF16)


def project(mine, theirs, places, w, after):
    width = w.shape[0]
    first = pl.BlockSpec((None, BLK, HALF), lambda p: (places[0], 0, 0))
    second = pl.BlockSpec((None, BLK, HALF), lambda p: (places[1], 0, 0))
    out = pl.BlockSpec((BLK, ROWS), lambda p: (0, p))
    return pl.pallas_call(
        project_kernel,
        grid=(width // ROWS,),
        in_specs=[first, second, pl.BlockSpec((ROWS, HALF), lambda p: (p, 0))] + [ANY] * len(after),
        out_specs=[out, out],
        out_shape=[jax.ShapeDtypeStruct((BLK, width), F32), jax.ShapeDtypeStruct((BLK, width), BF16)],
        compiler_params=pltpu.CompilerParams(vmem_limit_bytes=VMEM),
        cost_estimate=pl.CostEstimate(
            flops=4 * BLK * width * HALF, bytes_accessed=width * HALF * 2 + BLK * width * 6, transcendentals=0
        ),
        name="project",
    )(mine, theirs, w, *after)


def one_head(info, q, keys, values, ga):
    ga_r = ga.astype(F32).T
    ga_t = ga_r.astype(BF16)
    raw = [lax.dot_general(k, q, ACROSS, preferred_element_type=F32) for k in keys]
    yield
    grad_weights = [jnp.dot(v, ga_t, preferred_element_type=F32) for v in values]
    scores = []
    for j in range(4):
        s = raw[j] * (SCALE * LOG2E)
        if j > 0:
            s = s + jnp.where(info[j - 1] > 0, 0.0, -jnp.inf).astype(F32)
        scores.append(s)
    top = functools.reduce(jnp.maximum, [jnp.max(s, axis=0, keepdims=True) for s in scores])
    exps = [jnp.exp2(s - top) for s in scores]
    total = functools.reduce(jnp.add, [jnp.sum(e, axis=0, keepdims=True) for e in exps])
    inverse = 1.0 / total
    weights = [e * inverse for e in exps]
    weights_b = [p.astype(BF16) for p in weights]
    yield
    att_t = jnp.zeros((HD, BLK), F32)
    for j in range(4):
        att_t += jnp.dot(values[j].T, weights_b[j], preferred_element_type=F32)
    att_r = att_t.astype(BF16).astype(F32)
    attended = att_r.T.astype(BF16)
    delta = jnp.sum(ga_r * att_r, axis=0, keepdims=True)
    value_terms = [jnp.dot(p, ga, preferred_element_type=F32).astype(BF16) for p in weights_b]
    yield
    gq_t = jnp.zeros((HD, BLK), F32)
    key_terms = []
    for j in range(4):
        gs = (weights[j] * (grad_weights[j] - delta)).astype(BF16)
        gq_t += jnp.dot(keys[j].T, gs, preferred_element_type=F32)
        key_terms.append((jnp.dot(gs, q, preferred_element_type=F32) * SCALE).astype(BF16))
    yield attended, (gq_t * SCALE).T.astype(BF16), key_terms, value_terms


def attention_kernel(
    terms, rolled, info, q_ref, ko_ref, vo_ref, inner_ref, outer_ref, held_ref, theirs_ref, *rest
):
    ga_refs = rest[:terms]
    att_ref, gq_ref, own_ref, tin_ref, tout_ref, keep_ref, send_ref = rest[-7:]
    core, y = info[3], info[5]
    heads = []
    for a in range(PAIR):
        c = slice(a * HD, (a + 1) * HD)
        ga = functools.reduce(jnp.add, [ref[:, c].astype(F32) for ref in ga_refs]).astype(BF16)
        held, theirs = held_ref[:, c], theirs_ref[:, c]
        keys = [ko_ref[:, c], inner_ref[0, :, c], outer_ref[0, :, c], jnp.where(core == 0, held, theirs)]
        values = [vo_ref[:, c], inner_ref[1, :, c], outer_ref[1, :, c], jnp.where(core == 0, theirs, held)]
        heads.append(one_head(info, q_ref[:, c], keys, values, ga))
    for _ in range(3):
        for h in heads:
            next(h)
    for a in range(PAIR):
        c = slice(a * HD, (a + 1) * HD)
        attended, grad_query, key_terms, value_terms = next(heads[a])
        att_ref[:, c] = attended
        gq_ref[:, c] = grad_query
        for ref, j in ((own_ref, 0), (tin_ref, 1), (tout_ref, 2)):
            ref[0, :, c] = key_terms[j]
            ref[1, :, c] = value_terms[j]
        keep = jnp.where(core == 0, key_terms[3], value_terms[3])
        send = jnp.where(core == 0, value_terms[3], key_terms[3])
        for r in range(4):
            place = pl.multiple_of(lax.rem(y + r, 4) * PART, PART) if rolled else r * PART
            keep_ref[pl.ds(place, PART), c] = keep[r * PART : (r + 1) * PART]
            send_ref[pl.ds(place, PART), c] = send[r * PART : (r + 1) * PART]


def attention(part, begin, count, info, rows, ga, prior, after):
    wide = PAIR * HD
    whole = CHUNK // PAIR
    steps = count // PAIR
    first = begin // PAIR

    def head(t, info):
        return (0, info[6 + part] * whole + first + t)

    def heads(t, info):
        return (0, 0, info[6 + part] * whole + first + t)

    def col(t, *_):
        return (0, first + t)

    def pair(t, *_):
        return (0, 0, first + t)

    one = (BLK, wide)
    two = (2, BLK, wide)
    in_specs = (
        [pl.BlockSpec(one, head)] * 3
        + [pl.BlockSpec(two, heads)] * 2
        + [pl.BlockSpec(one, head)] * 2
        + [pl.BlockSpec(one, col)] * len(ga)
        + [ANY] * (len(prior) + len(after))
    )
    out_specs = (
        [pl.BlockSpec(one, head)] * 2 + [pl.BlockSpec(two, pair)] * 3 + [pl.BlockSpec(one, col)] * 2
    )
    full = jax.ShapeDtypeStruct((BLK, D), BF16)
    stacked = jax.ShapeDtypeStruct((2, BLK, CHUNK * HD), BF16)
    single = jax.ShapeDtypeStruct((BLK, CHUNK * HD), BF16)
    return pl.pallas_call(
        functools.partial(attention_kernel, len(ga), part == 0),
        grid_spec=pltpu.PrefetchScalarGridSpec(
            num_scalar_prefetch=1, grid=(steps,), in_specs=in_specs, out_specs=out_specs
        ),
        out_shape=[full, full, stacked, stacked, stacked, single, single],
        input_output_aliases={8 + len(ga) + i: i for i in range(len(prior))},
        compiler_params=pltpu.CompilerParams(vmem_limit_bytes=VMEM),
        cost_estimate=pl.CostEstimate(
            flops=count * 12 * BLK * 4 * BLK * HD,
            bytes_accessed=count * BLK * HD * 2 * 21,
            transcendentals=count * BLK * 4 * BLK,
        ),
        name="attention",
    )(info, *rows, *ga, *prior, *after)


def combine_kernel(info, own_ref, rin_ref, rout_ref, mine_ref, theirs_ref, *rest):
    gk_ref, gv_ref, total = rest[-3:]
    core, hit, y = info[3], info[4], info[5]
    total[...] = own_ref[...].astype(F32) + rin_ref[...].astype(F32) + rout_ref[...].astype(F32)

    @pl.when(hit > 0)
    def _():
        for r in range(4):
            place = pl.multiple_of(lax.rem(y + r, 4) * PART, PART)
            mine = mine_ref[r * PART : (r + 1) * PART].astype(F32)
            theirs = theirs_ref[r * PART : (r + 1) * PART].astype(F32)
            total[0, pl.ds(place, PART)] += jnp.where(core == 0, mine, theirs)
            total[1, pl.ds(place, PART)] += jnp.where(core == 0, theirs, mine)

    gk_ref[...] = total[0].astype(BF16)
    gv_ref[...] = total[1].astype(BF16)


def combine(part, info, own, rin, rout, sums, prior):
    wide = 4 * HD
    steps = CHUNK * HD // wide

    def head(t, info):
        return (0, info[6 + part] * steps + t)

    def col(t, *_):
        return (0, part * steps + t)

    def pair(t, *_):
        return (0, 0, t)

    two = pl.BlockSpec((2, BLK, wide), pair)
    one = pl.BlockSpec((BLK, wide), col)
    full = jax.ShapeDtypeStruct((BLK, D), BF16)
    return pl.pallas_call(
        combine_kernel,
        grid_spec=pltpu.PrefetchScalarGridSpec(
            num_scalar_prefetch=1,
            grid=(steps,),
            in_specs=[two, two, two, one, one] + [ANY] * len(prior),
            out_specs=[pl.BlockSpec((BLK, wide), head)] * 2,
            scratch_shapes=[pltpu.VMEM((2, BLK, wide), F32)],
        ),
        out_shape=[full, full],
        input_output_aliases={6: 0, 7: 1} if prior else {},
        compiler_params=pltpu.CompilerParams(vmem_limit_bytes=VMEM),
        cost_estimate=pl.CostEstimate(
            flops=CHUNK * BLK * HD * 8, bytes_accessed=CHUNK * BLK * HD * 2 * 10, transcendentals=0
        ),
        name="combine",
    )(info, own, rin, rout, *sums, *prior)


def add_kernel(a_ref, b_ref, *rest):
    rest[-1][...] = (a_ref[...].astype(F32) + b_ref[...].astype(F32)).astype(BF16)


def add(a, b, after=()):
    width = a.shape[1] // 2
    spec = pl.BlockSpec((a.shape[0], width), lambda t: (0, t))
    return pl.pallas_call(
        add_kernel,
        grid=(2,),
        in_specs=[spec, spec] + [ANY] * len(after),
        out_specs=spec,
        out_shape=jax.ShapeDtypeStruct(a.shape, BF16),
        compiler_params=pltpu.CompilerParams(vmem_limit_bytes=VMEM),
        cost_estimate=pl.CostEstimate(flops=a.size, bytes_accessed=a.size * 6, transcendentals=0),
        name="add",
    )(a, b, *after)


def gather_kernel(first_ref, *refs):
    total = functools.reduce(jnp.add, [ref[...].astype(F32) for ref in refs[:4]])
    width = first_ref.shape[1]
    refs[-1][:, :width] = first_ref[...]
    refs[-1][:, width:] = total.astype(BF16)


def gather(first, both, after):
    pieces = [both[:PART]] + [move(both[r * PART : (r + 1) * PART], "y", r, 4) for r in range(1, 4)]
    whole = pl.BlockSpec(memory_space=pltpu.VMEM)
    return pl.pallas_call(
        gather_kernel,
        in_specs=[whole] * 5 + [ANY] * len(after),
        out_specs=whole,
        out_shape=jax.ShapeDtypeStruct((PART, D), BF16),
        compiler_params=pltpu.CompilerParams(vmem_limit_bytes=VMEM),
        cost_estimate=pl.CostEstimate(
            flops=pieces[0].size * 4, bytes_accessed=pieces[0].size * 14, transcendentals=0
        ),
        name="gather",
    )(first, *pieces, *after)


def hold_kernel(*refs):
    del refs


def hold(x, after):
    return pl.pallas_call(
        hold_kernel,
        in_specs=[ANY] * (1 + len(after)),
        out_specs=ANY,
        out_shape=jax.ShapeDtypeStruct(x.shape, x.dtype),
        input_output_aliases={0: 0},
        cost_estimate=pl.CostEstimate(flops=0, bytes_accessed=0, transcendentals=0),
        name="hold",
    )(x, *after)


def pack_kernel(info, k_ref, v_ref, inner_ref, *outs):
    outs = outs[-4:]
    y, which = info[5], info[8]
    for r in range(4):
        rows = pl.ds(pl.multiple_of(lax.rem(y + r, 4) * PART, PART), PART)
        for i in range(4):

            @pl.when(which == i)
            def _():
                outs[r][...] = (k_ref, v_ref, inner_ref.at[0], inner_ref.at[1])[i][rows]


def pack(info, k, v, inner, after):
    def col(t, *_):
        return (0, t)

    wide = D // 2
    return pl.pallas_call(
        pack_kernel,
        grid_spec=pltpu.PrefetchScalarGridSpec(
            num_scalar_prefetch=1,
            grid=(2,),
            in_specs=[pl.BlockSpec((BLK, wide), col)] * 2
            + [pl.BlockSpec((2, BLK, wide), lambda t, *_: (0, 0, t))]
            + [ANY] * len(after),
            out_specs=[pl.BlockSpec((PART, wide), col)] * 4,
        ),
        out_shape=[jax.ShapeDtypeStruct((PART, D), BF16)] * 4,
        compiler_params=pltpu.CompilerParams(vmem_limit_bytes=VMEM),
        cost_estimate=pl.CostEstimate(flops=0, bytes_accessed=BLK * D * 10, transcendentals=0),
        name="pack",
    )(info, k, v, inner, *after)


def pick(which, pieces, after=()):
    count = len(pieces)

    def kernel(which, *refs):
        for i in range(count):

            @pl.when(which[0] == i)
            def _():
                refs[-1][...] = refs[i][...]

    spec = pl.BlockSpec(pieces[0].shape, lambda t, *_: (0, 0))
    return pl.pallas_call(
        kernel,
        grid_spec=pltpu.PrefetchScalarGridSpec(
            num_scalar_prefetch=1, grid=(1,), in_specs=[spec] * count + [ANY] * len(after), out_specs=spec
        ),
        out_shape=jax.ShapeDtypeStruct(pieces[0].shape, BF16),
        compiler_params=pltpu.CompilerParams(vmem_limit_bytes=VMEM),
        cost_estimate=pl.CostEstimate(flops=0, bytes_accessed=pieces[0].size * 10, transcendentals=0),
        name="pick",
    )(which[None].astype(jnp.int32), *pieces, *after)


def move(x, axis, step, size):
    return lax.ppermute(x, axis, [(i, (i + step) % size) for i in range(size)])


def swap_core(x):
    return move(x, "core", 1, 2)


def swap_outer(x):
    route = [(i, i + 1) for i in range(1, 15, 2)] + [(i + 1, i) for i in range(1, 15, 2)]
    return lax.ppermute(x, SKY, route)


def join_kernel(*refs):
    for r in range(4):
        refs[-1][r * PART : (r + 1) * PART] = refs[r][...]


def join(parts, after):
    wide = D // 2
    return pl.pallas_call(
        join_kernel,
        grid=(2,),
        in_specs=[pl.BlockSpec((PART, wide), lambda t: (0, t))] * 4 + [ANY] * len(after),
        out_specs=pl.BlockSpec((BLK, wide), lambda t: (0, t)),
        out_shape=jax.ShapeDtypeStruct((BLK, D), BF16),
        compiler_params=pltpu.CompilerParams(vmem_limit_bytes=VMEM),
        cost_estimate=pl.CostEstimate(flops=0, bytes_accessed=BLK * D * 4, transcendentals=0),
        name="join",
    )(*parts, *after)


def local(queries, key_states, value_states, key_blocks, global_block, w_out, grad_out):
    x, y, core = lax.axis_index("x_hi"), lax.axis_index("y"), lax.axis_index("core")
    side = lax.axis_index("x_lo")
    row = (x * 4 + y) * 2 + core
    root = global_block[0]
    ids = lax.dynamic_slice_in_dim(key_blocks, row, 1, 0)[0]
    above, below = ids[0], ids[1]
    inner_id = jnp.where(core == 0, below, above)
    outer_id = jnp.where(core == 0, above, below)
    live = (root != row) & (root != above) & (root != below)
    which = jnp.where(root % 2 == core, core, core + 2)
    info = jnp.stack(
        [inner_id >= 0, outer_id >= 0, live, core, root == row, y, side, 1 - side, which]
    ).astype(jnp.int32)
    q, k, v, go = queries[0], key_states[0], value_states[0], grad_out[0]
    w = lax.dynamic_slice_in_dim(w_out, core * HALF, HALF, 1)
    near = lax.all_gather(w, "z", axis=0, tiled=True)
    far = move(w, "x_lo", 1, 2)
    go_mine = lax.dynamic_slice_in_dim(go, core * HALF, HALF, 1)
    go_core = swap_core(lax.dynamic_slice_in_dim(go, (1 - core) * HALF, HALF, 1))
    kv = jnp.stack([k, v])
    inner = swap_core(kv)
    outer = swap_outer(kv)

    root_y, root_x = (root // 2) % 4, root // 8
    pieces = pack(info, k, v, inner, (go_core,))
    arrived = [pieces[0]] + [move(pieces[r], "y", r, 4) for r in range(1, 4)]
    mine = pick((y - root_y) % 4, arrived, (outer,))
    far = lax.all_gather(hold(far, (mine,)), "z", axis=0, tiled=True)
    ga_own, ga_core = project(go_mine[None], go_core[None], (0, 0), near, (arrived[1],))
    other = move(mine, "x_hi", 1, 2)
    quarter = pick((root_x - x) % 2, (mine, other), (ga_own,))
    held = join([quarter] + [move(quarter, "y", -r, 4) for r in range(1, 4)], ())
    rows = (q, k, v, inner, outer, held, swap_core(held))
    ga_near = (ga_own, swap_core(ga_core))

    out = attention(0, 0, CHUNK, info, rows, ga_near, (), ())
    att, gq, own0, tin0, tout0, keep, send = out
    ga_own, ga_core = project(go_mine[None], go_core[None], (0, 0), far, (held,))
    ga_far = (ga_own, swap_core(ga_core))
    rin0, rout0 = swap_core(tin0), swap_outer(tout0)
    both0 = add(keep, swap_core(send))
    quarter0 = lax.psum_scatter(both0, "y", scatter_dimension=0, tiled=True)

    out = attention(1, 0, CHUNK, info, rows, ga_far, (att, gq), (both0,))
    att, gq, own1, tin1, tout1, keep, send = out
    rin1, rout1 = swap_core(tin1), swap_outer(tout1)
    both1 = add(keep, swap_core(send), (rin0, rout0))
    quarters = gather(quarter0, both1, (rin1, rout1))
    halves = add(quarters, move(quarters, "x_hi", 1, 2))
    sums = join([halves] + [move(halves, "y", -r, 4) for r in range(1, 4)], ())
    sums = (sums, swap_core(sums))
    grads = combine(0, info, own0, rin0, rout0, sums, ())
    gk, gv = combine(1, info, own1, rin1, rout1, sums, grads)
    return tuple(a[None] for a in (att, gq, gk, gv))


def solution(mesh):
    inside = Mesh(mesh.devices.reshape(2, 4, 2, 4, 2), DP + SKY)
    rows = P(DP, SKY, None)
    return jax.shard_map(
        local,
        mesh=inside,
        in_specs=(rows, rows, rows, P(), P(), P(DP, None), rows),
        out_specs=(rows, rows, rows, rows),
        check_vma=False,
    )
```

```python
import functools
import math

import jax
import jax.numpy as jnp
from jax import lax
from jax.experimental import pallas as pl
from jax.experimental.pallas import tpu as pltpu
from jax.sharding import Mesh, PartitionSpec as P

HEADS = 24
HD = 128
BLK = 256
D = 3072
HALF = D // 2
PART = BLK // 4
ROWS = D // 8
PAIR = 2
SCALE = 1.0 / math.sqrt(HD)
LOG2E = 1.4426950408889634
DP = ("x_lo", "z")
SKY = ("x_hi", "y", "core")
CHUNK = 12
ACROSS = (((1,), (1,)), ((), ()))
F32 = jnp.float32
BF16 = jnp.bfloat16
VMEM = 60 * 2**20


ANY = pl.BlockSpec(memory_space=pl.ANY)


def project_kernel(mine_ref, theirs_ref, piece_ref, *rest):
    own_ref, send_ref = rest[-2:]
    piece = piece_ref[...]
    own_ref[...] = lax.dot_general(mine_ref[...], piece, ACROSS, preferred_element_type=F32)
    send_ref[...] = lax.dot_general(theirs_ref[...], piece, ACROSS, preferred_element_type=F32).astype(BF16)


def project(mine, theirs, places, w, after):
    width = w.shape[0]
    first = pl.BlockSpec((None, BLK, HALF), lambda p: (places[0], 0, 0))
    second = pl.BlockSpec((None, BLK, HALF), lambda p: (places[1], 0, 0))
    out = pl.BlockSpec((BLK, ROWS), lambda p: (0, p))
    return pl.pallas_call(
        project_kernel,
        grid=(width // ROWS,),
        in_specs=[first, second, pl.BlockSpec((ROWS, HALF), lambda p: (p, 0))] + [ANY] * len(after),
        out_specs=[out, out],
        out_shape=[jax.ShapeDtypeStruct((BLK, width), F32), jax.ShapeDtypeStruct((BLK, width), BF16)],
        compiler_params=pltpu.CompilerParams(vmem_limit_bytes=VMEM),
        cost_estimate=pl.CostEstimate(
            flops=4 * BLK * width * HALF, bytes_accessed=width * HALF * 2 + BLK * width * 6, transcendentals=0
        ),
        name="project",
    )(mine, theirs, w, *after)


def one_head(info, q, keys, values, ga):
    ga_r = ga.astype(F32).T
    ga_t = ga_r.astype(BF16)
    raw = [lax.dot_general(k, q, ACROSS, preferred_element_type=F32) for k in keys]
    yield
    grad_weights = [jnp.dot(v, ga_t, preferred_element_type=F32) for v in values]
    scores = []
    for j in range(4):
        s = raw[j] * (SCALE * LOG2E)
        if j > 0:
            s = s + jnp.where(info[j - 1] > 0, 0.0, -jnp.inf).astype(F32)
        scores.append(s)
    top = functools.reduce(jnp.maximum, [jnp.max(s, axis=0, keepdims=True) for s in scores])
    exps = [jnp.exp2(s - top) for s in scores]
    total = functools.reduce(jnp.add, [jnp.sum(e, axis=0, keepdims=True) for e in exps])
    inverse = 1.0 / total
    weights = [e * inverse for e in exps]
    weights_b = [p.astype(BF16) for p in weights]
    yield
    att_t = jnp.zeros((HD, BLK), F32)
    for j in range(4):
        att_t += jnp.dot(values[j].T, weights_b[j], preferred_element_type=F32)
    att_r = att_t.astype(BF16).astype(F32)
    attended = att_r.T.astype(BF16)
    delta = jnp.sum(ga_r * att_r, axis=0, keepdims=True)
    value_terms = [jnp.dot(p, ga, preferred_element_type=F32).astype(BF16) for p in weights_b]
    yield
    gq_t = jnp.zeros((HD, BLK), F32)
    key_terms = []
    for j in range(4):
        gs = (weights[j] * (grad_weights[j] - delta)).astype(BF16)
        gq_t += jnp.dot(keys[j].T, gs, preferred_element_type=F32)
        key_terms.append((jnp.dot(gs, q, preferred_element_type=F32) * SCALE).astype(BF16))
    yield attended, (gq_t * SCALE).T.astype(BF16), key_terms, value_terms


def attention_kernel(
    terms, rolled, info, q_ref, ko_ref, vo_ref, inner_ref, outer_ref, held_ref, theirs_ref, *rest
):
    ga_refs = rest[:terms]
    att_ref, gq_ref, own_ref, tin_ref, tout_ref, keep_ref, send_ref = rest[-7:]
    core, y = info[3], info[5]
    heads = []
    for a in range(PAIR):
        c = slice(a * HD, (a + 1) * HD)
        ga = functools.reduce(jnp.add, [ref[:, c].astype(F32) for ref in ga_refs]).astype(BF16)
        held, theirs = held_ref[:, c], theirs_ref[:, c]
        keys = [ko_ref[:, c], inner_ref[0, :, c], outer_ref[0, :, c], jnp.where(core == 0, held, theirs)]
        values = [vo_ref[:, c], inner_ref[1, :, c], outer_ref[1, :, c], jnp.where(core == 0, theirs, held)]
        heads.append(one_head(info, q_ref[:, c], keys, values, ga))
    for _ in range(3):
        for h in heads:
            next(h)
    for a in range(PAIR):
        c = slice(a * HD, (a + 1) * HD)
        attended, grad_query, key_terms, value_terms = next(heads[a])
        att_ref[:, c] = attended
        gq_ref[:, c] = grad_query
        for ref, j in ((own_ref, 0), (tin_ref, 1), (tout_ref, 2)):
            ref[0, :, c] = key_terms[j]
            ref[1, :, c] = value_terms[j]
        keep = jnp.where(core == 0, key_terms[3], value_terms[3])
        send = jnp.where(core == 0, value_terms[3], key_terms[3])
        for r in range(4):
            place = pl.multiple_of(lax.rem(y + r, 4) * PART, PART) if rolled else r * PART
            keep_ref[pl.ds(place, PART), c] = keep[r * PART : (r + 1) * PART]
            send_ref[pl.ds(place, PART), c] = send[r * PART : (r + 1) * PART]


def attention(part, begin, count, info, rows, ga, prior, after):
    wide = PAIR * HD
    whole = CHUNK // PAIR
    steps = count // PAIR
    first = begin // PAIR

    def head(t, info):
        return (0, info[6 + part] * whole + first + t)

    def heads(t, info):
        return (0, 0, info[6 + part] * whole + first + t)

    def col(t, *_):
        return (0, first + t)

    def pair(t, *_):
        return (0, 0, first + t)

    one = (BLK, wide)
    two = (2, BLK, wide)
    in_specs = (
        [pl.BlockSpec(one, head)] * 3
        + [pl.BlockSpec(two, heads)] * 2
        + [pl.BlockSpec(one, head)] * 2
        + [pl.BlockSpec(one, col)] * len(ga)
        + [ANY] * (len(prior) + len(after))
    )
    out_specs = (
        [pl.BlockSpec(one, head)] * 2 + [pl.BlockSpec(two, pair)] * 3 + [pl.BlockSpec(one, col)] * 2
    )
    full = jax.ShapeDtypeStruct((BLK, D), BF16)
    stacked = jax.ShapeDtypeStruct((2, BLK, CHUNK * HD), BF16)
    single = jax.ShapeDtypeStruct((BLK, CHUNK * HD), BF16)
    return pl.pallas_call(
        functools.partial(attention_kernel, len(ga), part == 0),
        grid_spec=pltpu.PrefetchScalarGridSpec(
            num_scalar_prefetch=1, grid=(steps,), in_specs=in_specs, out_specs=out_specs
        ),
        out_shape=[full, full, stacked, stacked, stacked, single, single],
        input_output_aliases={8 + len(ga) + i: i for i in range(len(prior))},
        compiler_params=pltpu.CompilerParams(vmem_limit_bytes=VMEM),
        cost_estimate=pl.CostEstimate(
            flops=count * 12 * BLK * 4 * BLK * HD,
            bytes_accessed=count * BLK * HD * 2 * 21,
            transcendentals=count * BLK * 4 * BLK,
        ),
        name="attention",
    )(info, *rows, *ga, *prior, *after)


def combine_kernel(info, own_ref, rin_ref, rout_ref, *rest):
    gk_ref, gv_ref = rest[-2:]
    total = own_ref[...].astype(F32) + rin_ref[...].astype(F32) + rout_ref[...].astype(F32)
    gk_ref[...] = total[0].astype(BF16)
    gv_ref[...] = total[1].astype(BF16)


def combine(part, info, own, rin, rout, prior, after):
    wide = 4 * HD
    steps = CHUNK * HD // wide
    two = pl.BlockSpec((2, BLK, wide), lambda t, *_: (0, 0, t))
    full = jax.ShapeDtypeStruct((BLK, D), BF16)
    return pl.pallas_call(
        combine_kernel,
        grid_spec=pltpu.PrefetchScalarGridSpec(
            num_scalar_prefetch=1,
            grid=(steps,),
            in_specs=[two, two, two] + [ANY] * (len(prior) + len(after)),
            out_specs=[pl.BlockSpec((BLK, wide), lambda t, info: (0, info[6 + part] * steps + t))] * 2,
        ),
        out_shape=[full, full],
        input_output_aliases={4: 0, 5: 1} if prior else {},
        compiler_params=pltpu.CompilerParams(vmem_limit_bytes=VMEM),
        cost_estimate=pl.CostEstimate(
            flops=CHUNK * BLK * HD * 4, bytes_accessed=CHUNK * BLK * HD * 2 * 8, transcendentals=0
        ),
        name="combine",
    )(info, own, rin, rout, *prior, *after)


def finish_kernel(info, mine_ref, theirs_ref, gk_ref, gv_ref, ok_ref, ov_ref):
    core, hit, y = info[3], info[4], info[5]
    ok_ref[...] = gk_ref[...]
    ov_ref[...] = gv_ref[...]

    @pl.when(hit > 0)
    def _():
        for r in range(4):
            rows = pl.ds(pl.multiple_of(lax.rem(y + r, 4) * PART, PART), PART)
            mine = mine_ref[r * PART : (r + 1) * PART].astype(F32)
            theirs = theirs_ref[r * PART : (r + 1) * PART].astype(F32)
            k_sum, v_sum = jnp.where(core == 0, mine, theirs), jnp.where(core == 0, theirs, mine)
            ok_ref[rows] = (gk_ref[rows].astype(F32) + k_sum).astype(BF16)
            ov_ref[rows] = (gv_ref[rows].astype(F32) + v_sum).astype(BF16)


def finish(info, mine, theirs, gk, gv):
    wide = 4 * HD
    steps = CHUNK * HD // wide

    def head(t, info):
        return (0, lax.rem(info[6] * steps + t, 2 * steps))

    here = pl.BlockSpec((BLK, wide), head)
    sums = pl.BlockSpec((BLK, wide), lambda t, *_: (0, t))
    full = jax.ShapeDtypeStruct((BLK, D), BF16)
    return pl.pallas_call(
        finish_kernel,
        grid_spec=pltpu.PrefetchScalarGridSpec(
            num_scalar_prefetch=1, grid=(2 * steps,), in_specs=[sums, sums, here, here], out_specs=[here, here]
        ),
        out_shape=[full, full],
        input_output_aliases={3: 0, 4: 1},
        compiler_params=pltpu.CompilerParams(vmem_limit_bytes=VMEM),
        cost_estimate=pl.CostEstimate(flops=BLK * D * 2, bytes_accessed=BLK * D * 12, transcendentals=0),
        name="finish",
    )(info, mine, theirs, gk, gv)


def add_kernel(a_ref, b_ref, *rest):
    rest[-1][...] = (a_ref[...].astype(F32) + b_ref[...].astype(F32)).astype(BF16)


def add(a, b, after=()):
    width = a.shape[1] // 2
    spec = pl.BlockSpec((a.shape[0], width), lambda t: (0, t))
    return pl.pallas_call(
        add_kernel,
        grid=(2,),
        in_specs=[spec, spec] + [ANY] * len(after),
        out_specs=spec,
        out_shape=jax.ShapeDtypeStruct(a.shape, BF16),
        compiler_params=pltpu.CompilerParams(vmem_limit_bytes=VMEM),
        cost_estimate=pl.CostEstimate(flops=a.size, bytes_accessed=a.size * 6, transcendentals=0),
        name="add",
    )(a, b, *after)


def split_kernel(a_ref, b_ref, *rest):
    for r in range(4):
        rows = slice(r * PART, (r + 1) * PART)
        rest[-4 + r][...] = (a_ref[rows].astype(F32) + b_ref[rows].astype(F32)).astype(BF16)


def split(a, b, after):
    width = a.shape[1] // 2
    spec = pl.BlockSpec((BLK, width), lambda t: (0, t))
    return pl.pallas_call(
        split_kernel,
        grid=(2,),
        in_specs=[spec, spec] + [ANY] * len(after),
        out_specs=[pl.BlockSpec((PART, width), lambda t: (0, t))] * 4,
        out_shape=[jax.ShapeDtypeStruct((PART, a.shape[1]), BF16)] * 4,
        compiler_params=pltpu.CompilerParams(vmem_limit_bytes=VMEM),
        cost_estimate=pl.CostEstimate(flops=a.size, bytes_accessed=a.size * 6, transcendentals=0),
        name="split",
    )(a, b, *after)


def gather_kernel(first_ref, *refs):
    total = functools.reduce(jnp.add, [ref[...].astype(F32) for ref in refs[:4]])
    width = first_ref.shape[1]
    refs[-1][:, :width] = first_ref[...]
    refs[-1][:, width:] = total.astype(BF16)


def gather(first, pieces, after):
    pieces = [pieces[0]] + [move(pieces[r], "y", r, 4) for r in range(1, 4)]
    whole = pl.BlockSpec(memory_space=pltpu.VMEM)
    return pl.pallas_call(
        gather_kernel,
        in_specs=[whole] * 5 + [ANY] * len(after),
        out_specs=whole,
        out_shape=jax.ShapeDtypeStruct((PART, D), BF16),
        compiler_params=pltpu.CompilerParams(vmem_limit_bytes=VMEM),
        cost_estimate=pl.CostEstimate(
            flops=pieces[0].size * 4, bytes_accessed=pieces[0].size * 14, transcendentals=0
        ),
        name="gather",
    )(first, *pieces, *after)


def hold_kernel(*refs):
    del refs


def hold(x, after):
    return pl.pallas_call(
        hold_kernel,
        in_specs=[ANY] * (1 + len(after)),
        out_specs=ANY,
        out_shape=jax.ShapeDtypeStruct(x.shape, x.dtype),
        input_output_aliases={0: 0},
        cost_estimate=pl.CostEstimate(flops=0, bytes_accessed=0, transcendentals=0),
        name="hold",
    )(x, *after)


def pack_kernel(info, k_ref, v_ref, inner_ref, *outs):
    outs = outs[-4:]
    y, which = info[5], info[8]
    for r in range(4):
        rows = pl.ds(pl.multiple_of(lax.rem(y + r, 4) * PART, PART), PART)
        for i in range(4):

            @pl.when(which == i)
            def _():
                outs[r][...] = (k_ref, v_ref, inner_ref.at[0], inner_ref.at[1])[i][rows]


def pack(info, k, v, inner, after):
    def col(t, *_):
        return (0, t)

    wide = D // 2
    return pl.pallas_call(
        pack_kernel,
        grid_spec=pltpu.PrefetchScalarGridSpec(
            num_scalar_prefetch=1,
            grid=(2,),
            in_specs=[pl.BlockSpec((BLK, wide), col)] * 2
            + [pl.BlockSpec((2, BLK, wide), lambda t, *_: (0, 0, t))]
            + [ANY] * len(after),
            out_specs=[pl.BlockSpec((PART, wide), col)] * 4,
        ),
        out_shape=[jax.ShapeDtypeStruct((PART, D), BF16)] * 4,
        compiler_params=pltpu.CompilerParams(vmem_limit_bytes=VMEM),
        cost_estimate=pl.CostEstimate(flops=0, bytes_accessed=BLK * D * 10, transcendentals=0),
        name="pack",
    )(info, k, v, inner, *after)


def pick(which, pieces, after=()):
    count = len(pieces)

    def kernel(which, *refs):
        for i in range(count):

            @pl.when(which[0] == i)
            def _():
                refs[-1][...] = refs[i][...]

    spec = pl.BlockSpec(pieces[0].shape, lambda t, *_: (0, 0))
    return pl.pallas_call(
        kernel,
        grid_spec=pltpu.PrefetchScalarGridSpec(
            num_scalar_prefetch=1, grid=(1,), in_specs=[spec] * count + [ANY] * len(after), out_specs=spec
        ),
        out_shape=jax.ShapeDtypeStruct(pieces[0].shape, BF16),
        compiler_params=pltpu.CompilerParams(vmem_limit_bytes=VMEM),
        cost_estimate=pl.CostEstimate(flops=0, bytes_accessed=pieces[0].size * 10, transcendentals=0),
        name="pick",
    )(which[None].astype(jnp.int32), *pieces, *after)


def move(x, axis, step, size):
    return lax.ppermute(x, axis, [(i, (i + step) % size) for i in range(size)])


def swap_core(x):
    return move(x, "core", 1, 2)


def swap_outer(x):
    route = [(i, i + 1) for i in range(1, 15, 2)] + [(i + 1, i) for i in range(1, 15, 2)]
    return lax.ppermute(x, SKY, route)


def join_kernel(*refs):
    for r in range(4):
        refs[-1][r * PART : (r + 1) * PART] = refs[r][...]


def join(parts, after):
    wide = D // 2
    return pl.pallas_call(
        join_kernel,
        grid=(2,),
        in_specs=[pl.BlockSpec((PART, wide), lambda t: (0, t))] * 4 + [ANY] * len(after),
        out_specs=pl.BlockSpec((BLK, wide), lambda t: (0, t)),
        out_shape=jax.ShapeDtypeStruct((BLK, D), BF16),
        compiler_params=pltpu.CompilerParams(vmem_limit_bytes=VMEM),
        cost_estimate=pl.CostEstimate(flops=0, bytes_accessed=BLK * D * 4, transcendentals=0),
        name="join",
    )(*parts, *after)


def local(queries, key_states, value_states, key_blocks, global_block, w_out, grad_out):
    x, y, core = lax.axis_index("x_hi"), lax.axis_index("y"), lax.axis_index("core")
    side = lax.axis_index("x_lo")
    row = (x * 4 + y) * 2 + core
    root = global_block[0]
    ids = lax.dynamic_slice_in_dim(key_blocks, row, 1, 0)[0]
    above, below = ids[0], ids[1]
    inner_id = jnp.where(core == 0, below, above)
    outer_id = jnp.where(core == 0, above, below)
    live = (root != row) & (root != above) & (root != below)
    which = jnp.where(root % 2 == core, core, core + 2)
    info = jnp.stack(
        [inner_id >= 0, outer_id >= 0, live, core, root == row, y, side, 1 - side, which]
    ).astype(jnp.int32)
    q, k, v, go = queries[0], key_states[0], value_states[0], grad_out[0]
    w = lax.dynamic_slice_in_dim(w_out, core * HALF, HALF, 1)
    near = lax.all_gather(w, "z", axis=0, tiled=True)
    go_mine = lax.dynamic_slice_in_dim(go, core * HALF, HALF, 1)
    go_core = swap_core(lax.dynamic_slice_in_dim(go, (1 - core) * HALF, HALF, 1))
    kv = jnp.stack([k, v])
    inner = swap_core(kv)
    outer = swap_outer(kv)
    far = move(w, "x_lo", 1, 2)

    root_y, root_x = (root // 2) % 4, root // 8
    pieces = pack(info, k, v, inner, (go_core,))
    arrived = [pieces[0]] + [move(pieces[r], "y", r, 4) for r in range(1, 4)]
    mine = pick((y - root_y) % 4, arrived, (outer,))
    far = lax.all_gather(hold(far, (mine,)), "z", axis=0, tiled=True)
    ga_own, ga_core = project(go_mine[None], go_core[None], (0, 0), near, (arrived[1],))
    other = move(mine, "x_hi", 1, 2)
    quarter = pick((root_x - x) % 2, (mine, other), (ga_own,))
    held = join([quarter] + [move(quarter, "y", -r, 4) for r in range(1, 4)], ())
    rows = (q, k, v, inner, outer, held, swap_core(held))
    ga_near = (ga_own, swap_core(ga_core))

    out = attention(0, 0, CHUNK, info, rows, ga_near, (), ())
    att, gq, own0, tin0, tout0, keep, send = out
    ga_own, ga_core = project(go_mine[None], go_core[None], (0, 0), far, (held,))
    ga_far = (ga_own, swap_core(ga_core))
    rin0, rout0 = swap_core(tin0), swap_outer(tout0)
    both0 = add(keep, swap_core(send))
    quarter0 = lax.psum_scatter(both0, "y", scatter_dimension=0, tiled=True)

    out = attention(1, 0, CHUNK, info, rows, ga_far, (att, gq), (both0,))
    att, gq, own1, tin1, tout1, keep, send = out
    rin1, rout1 = swap_core(tin1), swap_outer(tout1)
    both1 = split(keep, swap_core(send), (rin0, rout0))
    quarters = gather(quarter0, both1, (rin1, rout1))
    halves = add(quarters, move(quarters, "x_hi", 1, 2))
    grads = combine(0, info, own0, rin0, rout0, (), (quarters,))
    grads = combine(1, info, own1, rin1, rout1, grads, (halves,))
    sums = join([halves] + [move(halves, "y", -r, 4) for r in range(1, 4)], grads)
    gk, gv = finish(info, sums, swap_core(sums), *grads)
    return tuple(a[None] for a in (att, gq, gk, gv))


def solution(mesh):
    inside = Mesh(mesh.devices.reshape(2, 4, 2, 4, 2), DP + SKY)
    rows = P(DP, SKY, None)
    return jax.shard_map(
        local,
        mesh=inside,
        in_specs=(rows, rows, rows, P(), P(), P(DP, None), rows),
        out_specs=(rows, rows, rows, rows),
        check_vma=False,
    )
```

```python
import functools
import math

import jax
import jax.numpy as jnp
from jax import lax
from jax.experimental import pallas as pl
from jax.experimental.pallas import tpu as pltpu
from jax.sharding import Mesh, PartitionSpec as P

HEADS = 24
HD = 128
BLK = 256
D = 3072
HALF = D // 2
PART = BLK // 4
ROWS = D // 8
PAIR = 2
SCALE = 1.0 / math.sqrt(HD)
LOG2E = 1.4426950408889634
DP = ("x_lo", "z")
SKY = ("x_hi", "y", "core")
CHUNK = 12
ACROSS = (((1,), (1,)), ((), ()))
F32 = jnp.float32
BF16 = jnp.bfloat16
VMEM = 60 * 2**20


ANY = pl.BlockSpec(memory_space=pl.ANY)


def project_kernel(mine_ref, theirs_ref, piece_ref, *rest):
    own_ref, send_ref = rest[-2:]
    piece = piece_ref[...]
    own_ref[...] = lax.dot_general(mine_ref[...], piece, ACROSS, preferred_element_type=F32)
    send_ref[...] = lax.dot_general(theirs_ref[...], piece, ACROSS, preferred_element_type=F32).astype(BF16)


def project(mine, theirs, places, w, after):
    width = w.shape[0]
    first = pl.BlockSpec((None, BLK, HALF), lambda p: (places[0], 0, 0))
    second = pl.BlockSpec((None, BLK, HALF), lambda p: (places[1], 0, 0))
    out = pl.BlockSpec((BLK, ROWS), lambda p: (0, p))
    return pl.pallas_call(
        project_kernel,
        grid=(width // ROWS,),
        in_specs=[first, second, pl.BlockSpec((ROWS, HALF), lambda p: (p, 0))] + [ANY] * len(after),
        out_specs=[out, out],
        out_shape=[jax.ShapeDtypeStruct((BLK, width), F32), jax.ShapeDtypeStruct((BLK, width), BF16)],
        compiler_params=pltpu.CompilerParams(vmem_limit_bytes=VMEM),
        cost_estimate=pl.CostEstimate(
            flops=4 * BLK * width * HALF, bytes_accessed=width * HALF * 2 + BLK * width * 6, transcendentals=0
        ),
        name="project",
    )(mine, theirs, w, *after)


def one_head(info, q, keys, values, ga):
    ga_r = ga.astype(F32).T
    ga_t = ga_r.astype(BF16)
    raw = [lax.dot_general(k, q, ACROSS, preferred_element_type=F32) for k in keys]
    yield
    grad_weights = [jnp.dot(v, ga_t, preferred_element_type=F32) for v in values]
    scores = []
    for j in range(4):
        s = raw[j] * (SCALE * LOG2E)
        if j > 0:
            s = s + jnp.where(info[j - 1] > 0, 0.0, -jnp.inf).astype(F32)
        scores.append(s)
    top = functools.reduce(jnp.maximum, [jnp.max(s, axis=0, keepdims=True) for s in scores])
    exps = [jnp.exp2(s - top) for s in scores]
    total = functools.reduce(jnp.add, [jnp.sum(e, axis=0, keepdims=True) for e in exps])
    inverse = 1.0 / total
    weights = [e * inverse for e in exps]
    weights_b = [p.astype(BF16) for p in weights]
    yield
    att_t = jnp.zeros((HD, BLK), F32)
    for j in range(4):
        att_t += jnp.dot(values[j].T, weights_b[j], preferred_element_type=F32)
    att_r = att_t.astype(BF16).astype(F32)
    attended = att_r.T.astype(BF16)
    delta = jnp.sum(ga_r * att_r, axis=0, keepdims=True)
    value_terms = [jnp.dot(p, ga, preferred_element_type=F32).astype(BF16) for p in weights_b]
    yield
    gq_t = jnp.zeros((HD, BLK), F32)
    key_terms = []
    for j in range(4):
        gs = (weights[j] * (grad_weights[j] - delta)).astype(BF16)
        gq_t += jnp.dot(keys[j].T, gs, preferred_element_type=F32)
        key_terms.append((jnp.dot(gs, q, preferred_element_type=F32) * SCALE).astype(BF16))
    yield attended, (gq_t * SCALE).T.astype(BF16), key_terms, value_terms


def attention_kernel(
    terms, rolled, info, q_ref, ko_ref, vo_ref, inner_ref, outer_ref, held_ref, theirs_ref, *rest
):
    ga_refs = rest[:terms]
    att_ref, gq_ref, own_ref, tin_ref, tout_ref, keep_ref, send_ref = rest[-7:]
    core, y = info[3], info[5]
    heads = []
    for a in range(PAIR):
        c = slice(a * HD, (a + 1) * HD)
        ga = functools.reduce(jnp.add, [ref[:, c].astype(F32) for ref in ga_refs]).astype(BF16)
        held, theirs = held_ref[:, c], theirs_ref[:, c]
        keys = [ko_ref[:, c], inner_ref[0, :, c], outer_ref[0, :, c], jnp.where(core == 0, held, theirs)]
        values = [vo_ref[:, c], inner_ref[1, :, c], outer_ref[1, :, c], jnp.where(core == 0, theirs, held)]
        heads.append(one_head(info, q_ref[:, c], keys, values, ga))
    for _ in range(3):
        for h in heads:
            next(h)
    for a in range(PAIR):
        c = slice(a * HD, (a + 1) * HD)
        attended, grad_query, key_terms, value_terms = next(heads[a])
        att_ref[:, c] = attended
        gq_ref[:, c] = grad_query
        for ref, j in ((own_ref, 0), (tin_ref, 1), (tout_ref, 2)):
            ref[0, :, c] = key_terms[j]
            ref[1, :, c] = value_terms[j]
        keep = jnp.where(core == 0, key_terms[3], value_terms[3])
        send = jnp.where(core == 0, value_terms[3], key_terms[3])
        for r in range(4):
            place = pl.multiple_of(lax.rem(y + r, 4) * PART, PART) if rolled else r * PART
            keep_ref[pl.ds(place, PART), c] = keep[r * PART : (r + 1) * PART]
            send_ref[pl.ds(place, PART), c] = send[r * PART : (r + 1) * PART]


def attention(part, begin, count, info, rows, ga, prior, after):
    wide = PAIR * HD
    whole = CHUNK // PAIR
    steps = count // PAIR
    first = begin // PAIR

    def head(t, info):
        return (0, info[6 + part] * whole + first + t)

    def heads(t, info):
        return (0, 0, info[6 + part] * whole + first + t)

    def col(t, *_):
        return (0, first + t)

    def pair(t, *_):
        return (0, 0, first + t)

    one = (BLK, wide)
    two = (2, BLK, wide)
    in_specs = (
        [pl.BlockSpec(one, head)] * 3
        + [pl.BlockSpec(two, heads)] * 2
        + [pl.BlockSpec(one, head)] * 2
        + [pl.BlockSpec(one, col)] * len(ga)
        + [ANY] * (len(prior) + len(after))
    )
    out_specs = (
        [pl.BlockSpec(one, head)] * 2 + [pl.BlockSpec(two, pair)] * 3 + [pl.BlockSpec(one, col)] * 2
    )
    full = jax.ShapeDtypeStruct((BLK, D), BF16)
    stacked = jax.ShapeDtypeStruct((2, BLK, CHUNK * HD), BF16)
    single = jax.ShapeDtypeStruct((BLK, CHUNK * HD), BF16)
    return pl.pallas_call(
        functools.partial(attention_kernel, len(ga), part == 0),
        grid_spec=pltpu.PrefetchScalarGridSpec(
            num_scalar_prefetch=1, grid=(steps,), in_specs=in_specs, out_specs=out_specs
        ),
        out_shape=[full, full, stacked, stacked, stacked, single, single],
        input_output_aliases={8 + len(ga) + i: i for i in range(len(prior))},
        compiler_params=pltpu.CompilerParams(vmem_limit_bytes=VMEM),
        cost_estimate=pl.CostEstimate(
            flops=count * 12 * BLK * 4 * BLK * HD,
            bytes_accessed=count * BLK * HD * 2 * 21,
            transcendentals=count * BLK * 4 * BLK,
        ),
        name="attention",
    )(info, *rows, *ga, *prior, *after)


def combine_kernel(info, own_ref, rin_ref, rout_ref, *rest):
    gk_ref, gv_ref = rest[-2:]
    total = own_ref[...].astype(F32) + rin_ref[...].astype(F32) + rout_ref[...].astype(F32)
    gk_ref[...] = total[0].astype(BF16)
    gv_ref[...] = total[1].astype(BF16)


def combine(part, info, own, rin, rout, prior, after):
    wide = 4 * HD
    steps = CHUNK * HD // wide
    two = pl.BlockSpec((2, BLK, wide), lambda t, *_: (0, 0, t))
    full = jax.ShapeDtypeStruct((BLK, D), BF16)
    return pl.pallas_call(
        combine_kernel,
        grid_spec=pltpu.PrefetchScalarGridSpec(
            num_scalar_prefetch=1,
            grid=(steps,),
            in_specs=[two, two, two] + [ANY] * (len(prior) + len(after)),
            out_specs=[pl.BlockSpec((BLK, wide), lambda t, info: (0, info[6 + part] * steps + t))] * 2,
        ),
        out_shape=[full, full],
        input_output_aliases={4: 0, 5: 1} if prior else {},
        compiler_params=pltpu.CompilerParams(vmem_limit_bytes=VMEM),
        cost_estimate=pl.CostEstimate(
            flops=CHUNK * BLK * HD * 4, bytes_accessed=CHUNK * BLK * HD * 2 * 8, transcendentals=0
        ),
        name="combine",
    )(info, own, rin, rout, *prior, *after)


def finish_kernel(info, *refs):
    gk_ref, gv_ref, ok_ref, ov_ref = refs[8:]
    core, hit, y = info[3], info[4], info[5]
    ok_ref[...] = gk_ref[...]
    ov_ref[...] = gv_ref[...]

    @pl.when(hit > 0)
    def _():
        for r in range(4):
            rows = pl.ds(pl.multiple_of(lax.rem(y + r, 4) * PART, PART), PART)
            mine, theirs = refs[r][...].astype(F32), refs[4 + r][...].astype(F32)
            k_sum, v_sum = jnp.where(core == 0, mine, theirs), jnp.where(core == 0, theirs, mine)
            ok_ref[rows] = (gk_ref[rows].astype(F32) + k_sum).astype(BF16)
            ov_ref[rows] = (gv_ref[rows].astype(F32) + v_sum).astype(BF16)


def finish(info, mine, theirs, gk, gv):
    wide = 4 * HD
    steps = CHUNK * HD // wide

    def head(t, info):
        return (0, lax.rem(info[6] * steps + t, 2 * steps))

    here = pl.BlockSpec((BLK, wide), head)
    sums = pl.BlockSpec((PART, wide), lambda t, *_: (0, t))
    full = jax.ShapeDtypeStruct((BLK, D), BF16)
    return pl.pallas_call(
        finish_kernel,
        grid_spec=pltpu.PrefetchScalarGridSpec(
            num_scalar_prefetch=1, grid=(2 * steps,), in_specs=[sums] * 8 + [here, here], out_specs=[here, here]
        ),
        out_shape=[full, full],
        input_output_aliases={9: 0, 10: 1},
        compiler_params=pltpu.CompilerParams(vmem_limit_bytes=VMEM),
        cost_estimate=pl.CostEstimate(flops=BLK * D * 2, bytes_accessed=BLK * D * 12, transcendentals=0),
        name="finish",
    )(info, *mine, *theirs, gk, gv)


def add_kernel(a_ref, b_ref, *rest):
    rest[-1][...] = (a_ref[...].astype(F32) + b_ref[...].astype(F32)).astype(BF16)


def add(a, b, after=()):
    width = a.shape[1] // 2
    spec = pl.BlockSpec((a.shape[0], width), lambda t: (0, t))
    return pl.pallas_call(
        add_kernel,
        grid=(2,),
        in_specs=[spec, spec] + [ANY] * len(after),
        out_specs=spec,
        out_shape=jax.ShapeDtypeStruct(a.shape, BF16),
        compiler_params=pltpu.CompilerParams(vmem_limit_bytes=VMEM),
        cost_estimate=pl.CostEstimate(flops=a.size, bytes_accessed=a.size * 6, transcendentals=0),
        name="add",
    )(a, b, *after)


def split_kernel(a_ref, b_ref, *rest):
    for r in range(4):
        rows = slice(r * PART, (r + 1) * PART)
        rest[-4 + r][...] = (a_ref[rows].astype(F32) + b_ref[rows].astype(F32)).astype(BF16)


def split(a, b, after):
    width = a.shape[1] // 2
    spec = pl.BlockSpec((BLK, width), lambda t: (0, t))
    return pl.pallas_call(
        split_kernel,
        grid=(2,),
        in_specs=[spec, spec] + [ANY] * len(after),
        out_specs=[pl.BlockSpec((PART, width), lambda t: (0, t))] * 4,
        out_shape=[jax.ShapeDtypeStruct((PART, a.shape[1]), BF16)] * 4,
        compiler_params=pltpu.CompilerParams(vmem_limit_bytes=VMEM),
        cost_estimate=pl.CostEstimate(flops=a.size, bytes_accessed=a.size * 6, transcendentals=0),
        name="split",
    )(a, b, *after)


def gather_kernel(first_ref, *refs):
    total = functools.reduce(jnp.add, [ref[...].astype(F32) for ref in refs[:4]])
    width = first_ref.shape[1]
    refs[-1][:, :width] = first_ref[...]
    refs[-1][:, width:] = total.astype(BF16)


def gather(first, pieces, after):
    pieces = [pieces[0]] + [move(pieces[r], "y", r, 4) for r in range(1, 4)]
    whole = pl.BlockSpec(memory_space=pltpu.VMEM)
    return pl.pallas_call(
        gather_kernel,
        in_specs=[whole] * 5 + [ANY] * len(after),
        out_specs=whole,
        out_shape=jax.ShapeDtypeStruct((PART, D), BF16),
        compiler_params=pltpu.CompilerParams(vmem_limit_bytes=VMEM),
        cost_estimate=pl.CostEstimate(
            flops=pieces[0].size * 4, bytes_accessed=pieces[0].size * 14, transcendentals=0
        ),
        name="gather",
    )(first, *pieces, *after)


def hold_kernel(*refs):
    del refs


def hold(x, after):
    return pl.pallas_call(
        hold_kernel,
        in_specs=[ANY] * (1 + len(after)),
        out_specs=ANY,
        out_shape=jax.ShapeDtypeStruct(x.shape, x.dtype),
        input_output_aliases={0: 0},
        cost_estimate=pl.CostEstimate(flops=0, bytes_accessed=0, transcendentals=0),
        name="hold",
    )(x, *after)


def pack_kernel(info, k_ref, v_ref, inner_ref, *outs):
    outs = outs[-4:]
    y, which = info[5], info[8]
    for r in range(4):
        rows = pl.ds(pl.multiple_of(lax.rem(y + r, 4) * PART, PART), PART)
        for i in range(4):

            @pl.when(which == i)
            def _():
                outs[r][...] = (k_ref, v_ref, inner_ref.at[0], inner_ref.at[1])[i][rows]


def pack(info, k, v, inner, after):
    def col(t, *_):
        return (0, t)

    wide = D // 2
    return pl.pallas_call(
        pack_kernel,
        grid_spec=pltpu.PrefetchScalarGridSpec(
            num_scalar_prefetch=1,
            grid=(2,),
            in_specs=[pl.BlockSpec((BLK, wide), col)] * 2
            + [pl.BlockSpec((2, BLK, wide), lambda t, *_: (0, 0, t))]
            + [ANY] * len(after),
            out_specs=[pl.BlockSpec((PART, wide), col)] * 4,
        ),
        out_shape=[jax.ShapeDtypeStruct((PART, D), BF16)] * 4,
        compiler_params=pltpu.CompilerParams(vmem_limit_bytes=VMEM),
        cost_estimate=pl.CostEstimate(flops=0, bytes_accessed=BLK * D * 10, transcendentals=0),
        name="pack",
    )(info, k, v, inner, *after)


def pick(which, pieces, after=()):
    count = len(pieces)

    def kernel(which, *refs):
        for i in range(count):

            @pl.when(which[0] == i)
            def _():
                refs[-1][...] = refs[i][...]

    spec = pl.BlockSpec(pieces[0].shape, lambda t, *_: (0, 0))
    return pl.pallas_call(
        kernel,
        grid_spec=pltpu.PrefetchScalarGridSpec(
            num_scalar_prefetch=1, grid=(1,), in_specs=[spec] * count + [ANY] * len(after), out_specs=spec
        ),
        out_shape=jax.ShapeDtypeStruct(pieces[0].shape, BF16),
        compiler_params=pltpu.CompilerParams(vmem_limit_bytes=VMEM),
        cost_estimate=pl.CostEstimate(flops=0, bytes_accessed=pieces[0].size * 10, transcendentals=0),
        name="pick",
    )(which[None].astype(jnp.int32), *pieces, *after)


def move(x, axis, step, size):
    return lax.ppermute(x, axis, [(i, (i + step) % size) for i in range(size)])


def swap_core(x):
    return move(x, "core", 1, 2)


def swap_outer(x):
    route = [(i, i + 1) for i in range(1, 15, 2)] + [(i + 1, i) for i in range(1, 15, 2)]
    return lax.ppermute(x, SKY, route)


def join_kernel(*refs):
    for r in range(4):
        refs[-1][r * PART : (r + 1) * PART] = refs[r][...]


def join(parts, after):
    wide = D // 2
    return pl.pallas_call(
        join_kernel,
        grid=(2,),
        in_specs=[pl.BlockSpec((PART, wide), lambda t: (0, t))] * 4 + [ANY] * len(after),
        out_specs=pl.BlockSpec((BLK, wide), lambda t: (0, t)),
        out_shape=jax.ShapeDtypeStruct((BLK, D), BF16),
        compiler_params=pltpu.CompilerParams(vmem_limit_bytes=VMEM),
        cost_estimate=pl.CostEstimate(flops=0, bytes_accessed=BLK * D * 4, transcendentals=0),
        name="join",
    )(*parts, *after)


def local(queries, key_states, value_states, key_blocks, global_block, w_out, grad_out):
    x, y, core = lax.axis_index("x_hi"), lax.axis_index("y"), lax.axis_index("core")
    side = lax.axis_index("x_lo")
    row = (x * 4 + y) * 2 + core
    root = global_block[0]
    ids = lax.dynamic_slice_in_dim(key_blocks, row, 1, 0)[0]
    above, below = ids[0], ids[1]
    inner_id = jnp.where(core == 0, below, above)
    outer_id = jnp.where(core == 0, above, below)
    live = (root != row) & (root != above) & (root != below)
    which = jnp.where(root % 2 == core, core, core + 2)
    info = jnp.stack(
        [inner_id >= 0, outer_id >= 0, live, core, root == row, y, side, 1 - side, which]
    ).astype(jnp.int32)
    q, k, v, go = queries[0], key_states[0], value_states[0], grad_out[0]
    w = lax.dynamic_slice_in_dim(w_out, core * HALF, HALF, 1)
    near = lax.all_gather(w, "z", axis=0, tiled=True)
    go_mine = lax.dynamic_slice_in_dim(go, core * HALF, HALF, 1)
    go_core = swap_core(lax.dynamic_slice_in_dim(go, (1 - core) * HALF, HALF, 1))
    kv = jnp.stack([k, v])
    inner = swap_core(kv)
    outer = swap_outer(kv)
    far = move(w, "x_lo", 1, 2)

    root_y, root_x = (root // 2) % 4, root // 8
    pieces = pack(info, k, v, inner, (go_core,))
    arrived = [pieces[0]] + [move(pieces[r], "y", r, 4) for r in range(1, 4)]
    mine = pick((y - root_y) % 4, arrived, (outer,))
    far = lax.all_gather(hold(far, (mine,)), "z", axis=0, tiled=True)
    ga_own, ga_core = project(go_mine[None], go_core[None], (0, 0), near, (arrived[1],))
    other = move(mine, "x_hi", 1, 2)
    quarter = pick((root_x - x) % 2, (mine, other), (ga_own,))
    ga_near = (ga_own, swap_core(ga_core))
    held = join([quarter] + [move(quarter, "y", -r, 4) for r in range(1, 4)], ga_near)
    rows = (q, k, v, inner, outer, held, swap_core(held))

    out = attention(0, 0, CHUNK, info, rows, ga_near, (), ())
    att, gq, own0, tin0, tout0, keep, send = out
    ga_own, ga_core = project(go_mine[None], go_core[None], (0, 0), far, (held,))
    ga_far = (ga_own, swap_core(ga_core))
    rin0, rout0 = swap_core(tin0), swap_outer(tout0)
    both0 = add(keep, swap_core(send))
    quarter0 = lax.psum_scatter(both0, "y", scatter_dimension=0, tiled=True)

    out = attention(1, 0, CHUNK, info, rows, ga_far, (att, gq), (both0,))
    att, gq, own1, tin1, tout1, keep, send = out
    rin1, rout1 = swap_core(tin1), swap_outer(tout1)
    both1 = split(keep, swap_core(send), (rin0, rout0))
    quarters = gather(quarter0, both1, (rin1, rout1))
    halves = add(quarters, move(quarters, "x_hi", 1, 2))
    grads = combine(0, info, own0, rin0, rout0, (), (quarters,))
    grads = combine(1, info, own1, rin1, rout1, grads, (halves,))
    sums = [halves] + [move(halves, "y", -r, 4) for r in range(1, 4)]
    sums[2] = hold(sums[2], grads)
    gk, gv = finish(info, sums, [swap_core(s) for s in sums], *grads)
    return tuple(a[None] for a in (att, gq, gk, gv))


def solution(mesh):
    inside = Mesh(mesh.devices.reshape(2, 4, 2, 4, 2), DP + SKY)
    rows = P(DP, SKY, None)
    return jax.shard_map(
        local,
        mesh=inside,
        in_specs=(rows, rows, rows, P(), P(), P(DP, None), rows),
        out_specs=(rows, rows, rows, rows),
        check_vma=False,
    )
```

```python
import functools
import math

import jax
import jax.numpy as jnp
from jax import lax
from jax.experimental import pallas as pl
from jax.experimental.pallas import tpu as pltpu
from jax.sharding import Mesh, PartitionSpec as P

HEADS = 24
HD = 128
BLK = 256
D = 3072
HALF = D // 2
PART = BLK // 4
ROWS = D // 8
PAIR = 2
SCALE = 1.0 / math.sqrt(HD)
LOG2E = 1.4426950408889634
DP = ("x_lo", "z")
SKY = ("x_hi", "y", "core")
CHUNK = 12
ACROSS = (((1,), (1,)), ((), ()))
F32 = jnp.float32
BF16 = jnp.bfloat16
VMEM = 60 * 2**20


ANY = pl.BlockSpec(memory_space=pl.ANY)


def project_kernel(mine_ref, theirs_ref, piece_ref, *rest):
    own_ref, send_ref = rest[-2:]
    piece = piece_ref[...]
    own_ref[...] = lax.dot_general(mine_ref[...], piece, ACROSS, preferred_element_type=F32)
    send_ref[...] = lax.dot_general(theirs_ref[...], piece, ACROSS, preferred_element_type=F32).astype(BF16)


def project(mine, theirs, places, w, after):
    width = w.shape[0]
    first = pl.BlockSpec((None, BLK, HALF), lambda p: (places[0], 0, 0))
    second = pl.BlockSpec((None, BLK, HALF), lambda p: (places[1], 0, 0))
    out = pl.BlockSpec((BLK, ROWS), lambda p: (0, p))
    return pl.pallas_call(
        project_kernel,
        grid=(width // ROWS,),
        in_specs=[first, second, pl.BlockSpec((ROWS, HALF), lambda p: (p, 0))] + [ANY] * len(after),
        out_specs=[out, out],
        out_shape=[jax.ShapeDtypeStruct((BLK, width), F32), jax.ShapeDtypeStruct((BLK, width), BF16)],
        compiler_params=pltpu.CompilerParams(vmem_limit_bytes=VMEM),
        cost_estimate=pl.CostEstimate(
            flops=4 * BLK * width * HALF, bytes_accessed=width * HALF * 2 + BLK * width * 6, transcendentals=0
        ),
        name="project",
    )(mine, theirs, w, *after)


def one_head(info, q, keys, values, ga):
    ga_r = ga.astype(F32).T
    ga_t = ga_r.astype(BF16)
    raw = [lax.dot_general(k, q, ACROSS, preferred_element_type=F32) for k in keys]
    yield
    grad_weights = [jnp.dot(v, ga_t, preferred_element_type=F32) for v in values]
    scores = []
    for j in range(4):
        s = raw[j] * (SCALE * LOG2E)
        if j > 0:
            s = s + jnp.where(info[j - 1] > 0, 0.0, -jnp.inf).astype(F32)
        scores.append(s)
    top = functools.reduce(jnp.maximum, [jnp.max(s, axis=0, keepdims=True) for s in scores])
    exps = [jnp.exp2(s - top) for s in scores]
    total = functools.reduce(jnp.add, [jnp.sum(e, axis=0, keepdims=True) for e in exps])
    inverse = 1.0 / total
    weights = [e * inverse for e in exps]
    weights_b = [p.astype(BF16) for p in weights]
    yield
    att_t = jnp.zeros((HD, BLK), F32)
    for j in range(4):
        att_t += jnp.dot(values[j].T, weights_b[j], preferred_element_type=F32)
    att_r = att_t.astype(BF16).astype(F32)
    attended = att_r.T.astype(BF16)
    delta = jnp.sum(ga_r * att_r, axis=0, keepdims=True)
    value_terms = [jnp.dot(p, ga, preferred_element_type=F32).astype(BF16) for p in weights_b]
    yield
    gq_t = jnp.zeros((HD, BLK), F32)
    key_terms = []
    for j in range(4):
        gs = (weights[j] * (grad_weights[j] - delta)).astype(BF16)
        gq_t += jnp.dot(keys[j].T, gs, preferred_element_type=F32)
        key_terms.append((jnp.dot(gs, q, preferred_element_type=F32) * SCALE).astype(BF16))
    yield attended, (gq_t * SCALE).T.astype(BF16), key_terms, value_terms


def attention_kernel(
    terms, rolled, info, q_ref, ko_ref, vo_ref, inner_ref, outer_ref, *rest
):
    parts, ga_refs = rest[:8], rest[8 : 8 + terms]
    att_ref, gq_ref, own_ref, tin_ref, tout_ref, keep_ref, send_ref = rest[-7:]
    core, y = info[3], info[5]
    heads = []
    for a in range(PAIR):
        c = slice(a * HD, (a + 1) * HD)
        ga = functools.reduce(jnp.add, [ref[:, c].astype(F32) for ref in ga_refs]).astype(BF16)
        held = jnp.concatenate([ref[:, c] for ref in parts[:4]], axis=0)
        theirs = jnp.concatenate([ref[:, c] for ref in parts[4:]], axis=0)
        keys = [ko_ref[:, c], inner_ref[0, :, c], outer_ref[0, :, c], jnp.where(core == 0, held, theirs)]
        values = [vo_ref[:, c], inner_ref[1, :, c], outer_ref[1, :, c], jnp.where(core == 0, theirs, held)]
        heads.append(one_head(info, q_ref[:, c], keys, values, ga))
    for _ in range(3):
        for h in heads:
            next(h)
    for a in range(PAIR):
        c = slice(a * HD, (a + 1) * HD)
        attended, grad_query, key_terms, value_terms = next(heads[a])
        att_ref[:, c] = attended
        gq_ref[:, c] = grad_query
        for ref, j in ((own_ref, 0), (tin_ref, 1), (tout_ref, 2)):
            ref[0, :, c] = key_terms[j]
            ref[1, :, c] = value_terms[j]
        keep = jnp.where(core == 0, key_terms[3], value_terms[3])
        send = jnp.where(core == 0, value_terms[3], key_terms[3])
        for r in range(4):
            place = pl.multiple_of(lax.rem(y + r, 4) * PART, PART) if rolled else r * PART
            keep_ref[pl.ds(place, PART), c] = keep[r * PART : (r + 1) * PART]
            send_ref[pl.ds(place, PART), c] = send[r * PART : (r + 1) * PART]


def attention(part, begin, count, info, rows, ga, prior, after):
    wide = PAIR * HD
    whole = CHUNK // PAIR
    steps = count // PAIR
    first = begin // PAIR

    def head(t, info):
        return (0, info[6 + part] * whole + first + t)

    def heads(t, info):
        return (0, 0, info[6 + part] * whole + first + t)

    def col(t, *_):
        return (0, first + t)

    def pair(t, *_):
        return (0, 0, first + t)

    one = (BLK, wide)
    two = (2, BLK, wide)
    in_specs = (
        [pl.BlockSpec(one, head)] * 3
        + [pl.BlockSpec(two, heads)] * 2
        + [pl.BlockSpec((PART, wide), head)] * 8
        + [pl.BlockSpec(one, col)] * len(ga)
        + [ANY] * (len(prior) + len(after))
    )
    out_specs = (
        [pl.BlockSpec(one, head)] * 2 + [pl.BlockSpec(two, pair)] * 3 + [pl.BlockSpec(one, col)] * 2
    )
    full = jax.ShapeDtypeStruct((BLK, D), BF16)
    stacked = jax.ShapeDtypeStruct((2, BLK, CHUNK * HD), BF16)
    single = jax.ShapeDtypeStruct((BLK, CHUNK * HD), BF16)
    return pl.pallas_call(
        functools.partial(attention_kernel, len(ga), part == 0),
        grid_spec=pltpu.PrefetchScalarGridSpec(
            num_scalar_prefetch=1, grid=(steps,), in_specs=in_specs, out_specs=out_specs
        ),
        out_shape=[full, full, stacked, stacked, stacked, single, single],
        input_output_aliases={14 + len(ga) + i: i for i in range(len(prior))},
        compiler_params=pltpu.CompilerParams(vmem_limit_bytes=VMEM),
        cost_estimate=pl.CostEstimate(
            flops=count * 12 * BLK * 4 * BLK * HD,
            bytes_accessed=count * BLK * HD * 2 * 21,
            transcendentals=count * BLK * 4 * BLK,
        ),
        name="attention",
    )(info, *rows, *ga, *prior, *after)


def combine_kernel(info, own_ref, rin_ref, rout_ref, *rest):
    gk_ref, gv_ref = rest[-2:]
    total = own_ref[...].astype(F32) + rin_ref[...].astype(F32) + rout_ref[...].astype(F32)
    gk_ref[...] = total[0].astype(BF16)
    gv_ref[...] = total[1].astype(BF16)


def combine(part, info, own, rin, rout, prior, after):
    wide = 4 * HD
    steps = CHUNK * HD // wide
    two = pl.BlockSpec((2, BLK, wide), lambda t, *_: (0, 0, t))
    full = jax.ShapeDtypeStruct((BLK, D), BF16)
    return pl.pallas_call(
        combine_kernel,
        grid_spec=pltpu.PrefetchScalarGridSpec(
            num_scalar_prefetch=1,
            grid=(steps,),
            in_specs=[two, two, two] + [ANY] * (len(prior) + len(after)),
            out_specs=[pl.BlockSpec((BLK, wide), lambda t, info: (0, info[6 + part] * steps + t))] * 2,
        ),
        out_shape=[full, full],
        input_output_aliases={4: 0, 5: 1} if prior else {},
        compiler_params=pltpu.CompilerParams(vmem_limit_bytes=VMEM),
        cost_estimate=pl.CostEstimate(
            flops=CHUNK * BLK * HD * 4, bytes_accessed=CHUNK * BLK * HD * 2 * 8, transcendentals=0
        ),
        name="combine",
    )(info, own, rin, rout, *prior, *after)


def finish_kernel(info, *refs):
    gk_ref, gv_ref, ok_ref, ov_ref = refs[8:]
    core, hit, y = info[3], info[4], info[5]
    ok_ref[...] = gk_ref[...]
    ov_ref[...] = gv_ref[...]

    @pl.when(hit > 0)
    def _():
        for r in range(4):
            rows = pl.ds(pl.multiple_of(lax.rem(y + r, 4) * PART, PART), PART)
            mine, theirs = refs[r][...].astype(F32), refs[4 + r][...].astype(F32)
            k_sum, v_sum = jnp.where(core == 0, mine, theirs), jnp.where(core == 0, theirs, mine)
            ok_ref[rows] = (gk_ref[rows].astype(F32) + k_sum).astype(BF16)
            ov_ref[rows] = (gv_ref[rows].astype(F32) + v_sum).astype(BF16)


def finish(info, mine, theirs, gk, gv):
    wide = 4 * HD
    steps = CHUNK * HD // wide

    def head(t, info):
        return (0, lax.rem(info[6] * steps + t, 2 * steps))

    here = pl.BlockSpec((BLK, wide), head)
    sums = pl.BlockSpec((PART, wide), lambda t, *_: (0, t))
    full = jax.ShapeDtypeStruct((BLK, D), BF16)
    return pl.pallas_call(
        finish_kernel,
        grid_spec=pltpu.PrefetchScalarGridSpec(
            num_scalar_prefetch=1, grid=(2 * steps,), in_specs=[sums] * 8 + [here, here], out_specs=[here, here]
        ),
        out_shape=[full, full],
        input_output_aliases={9: 0, 10: 1},
        compiler_params=pltpu.CompilerParams(vmem_limit_bytes=VMEM),
        cost_estimate=pl.CostEstimate(flops=BLK * D * 2, bytes_accessed=BLK * D * 12, transcendentals=0),
        name="finish",
    )(info, *mine, *theirs, gk, gv)


def add_kernel(a_ref, b_ref, *rest):
    rest[-1][...] = (a_ref[...].astype(F32) + b_ref[...].astype(F32)).astype(BF16)


def add(a, b, after=()):
    width = a.shape[1] // 2
    spec = pl.BlockSpec((a.shape[0], width), lambda t: (0, t))
    return pl.pallas_call(
        add_kernel,
        grid=(2,),
        in_specs=[spec, spec] + [ANY] * len(after),
        out_specs=spec,
        out_shape=jax.ShapeDtypeStruct(a.shape, BF16),
        compiler_params=pltpu.CompilerParams(vmem_limit_bytes=VMEM),
        cost_estimate=pl.CostEstimate(flops=a.size, bytes_accessed=a.size * 6, transcendentals=0),
        name="add",
    )(a, b, *after)


def split_kernel(a_ref, b_ref, *rest):
    for r in range(4):
        rows = slice(r * PART, (r + 1) * PART)
        rest[-4 + r][...] = (a_ref[rows].astype(F32) + b_ref[rows].astype(F32)).astype(BF16)


def split(a, b, after):
    width = a.shape[1] // 2
    spec = pl.BlockSpec((BLK, width), lambda t: (0, t))
    return pl.pallas_call(
        split_kernel,
        grid=(2,),
        in_specs=[spec, spec] + [ANY] * len(after),
        out_specs=[pl.BlockSpec((PART, width), lambda t: (0, t))] * 4,
        out_shape=[jax.ShapeDtypeStruct((PART, a.shape[1]), BF16)] * 4,
        compiler_params=pltpu.CompilerParams(vmem_limit_bytes=VMEM),
        cost_estimate=pl.CostEstimate(flops=a.size, bytes_accessed=a.size * 6, transcendentals=0),
        name="split",
    )(a, b, *after)


def gather_kernel(first_ref, *refs):
    total = functools.reduce(jnp.add, [ref[...].astype(F32) for ref in refs[:4]])
    width = first_ref.shape[1]
    refs[-1][:, :width] = first_ref[...]
    refs[-1][:, width:] = total.astype(BF16)


def gather(first, pieces, after):
    pieces = [pieces[0]] + [move(pieces[r], "y", r, 4) for r in range(1, 4)]
    whole = pl.BlockSpec(memory_space=pltpu.VMEM)
    return pl.pallas_call(
        gather_kernel,
        in_specs=[whole] * 5 + [ANY] * len(after),
        out_specs=whole,
        out_shape=jax.ShapeDtypeStruct((PART, D), BF16),
        compiler_params=pltpu.CompilerParams(vmem_limit_bytes=VMEM),
        cost_estimate=pl.CostEstimate(
            flops=pieces[0].size * 4, bytes_accessed=pieces[0].size * 14, transcendentals=0
        ),
        name="gather",
    )(first, *pieces, *after)


def hold_kernel(*refs):
    del refs


def hold(x, after):
    return pl.pallas_call(
        hold_kernel,
        in_specs=[ANY] * (1 + len(after)),
        out_specs=ANY,
        out_shape=jax.ShapeDtypeStruct(x.shape, x.dtype),
        input_output_aliases={0: 0},
        cost_estimate=pl.CostEstimate(flops=0, bytes_accessed=0, transcendentals=0),
        name="hold",
    )(x, *after)


def pack_kernel(info, k_ref, v_ref, inner_ref, *outs):
    outs = outs[-4:]
    y, which = info[5], info[8]
    for r in range(4):
        rows = pl.ds(pl.multiple_of(lax.rem(y + r, 4) * PART, PART), PART)
        for i in range(4):

            @pl.when(which == i)
            def _():
                outs[r][...] = (k_ref, v_ref, inner_ref.at[0], inner_ref.at[1])[i][rows]


def pack(info, k, v, inner, after):
    def col(t, *_):
        return (0, t)

    wide = D // 2
    return pl.pallas_call(
        pack_kernel,
        grid_spec=pltpu.PrefetchScalarGridSpec(
            num_scalar_prefetch=1,
            grid=(2,),
            in_specs=[pl.BlockSpec((BLK, wide), col)] * 2
            + [pl.BlockSpec((2, BLK, wide), lambda t, *_: (0, 0, t))]
            + [ANY] * len(after),
            out_specs=[pl.BlockSpec((PART, wide), col)] * 4,
        ),
        out_shape=[jax.ShapeDtypeStruct((PART, D), BF16)] * 4,
        compiler_params=pltpu.CompilerParams(vmem_limit_bytes=VMEM),
        cost_estimate=pl.CostEstimate(flops=0, bytes_accessed=BLK * D * 10, transcendentals=0),
        name="pack",
    )(info, k, v, inner, *after)


def pick(which, pieces, after=()):
    count = len(pieces)

    def kernel(which, *refs):
        for i in range(count):

            @pl.when(which[0] == i)
            def _():
                refs[-1][...] = refs[i][...]

    spec = pl.BlockSpec(pieces[0].shape, lambda t, *_: (0, 0))
    return pl.pallas_call(
        kernel,
        grid_spec=pltpu.PrefetchScalarGridSpec(
            num_scalar_prefetch=1, grid=(1,), in_specs=[spec] * count + [ANY] * len(after), out_specs=spec
        ),
        out_shape=jax.ShapeDtypeStruct(pieces[0].shape, BF16),
        compiler_params=pltpu.CompilerParams(vmem_limit_bytes=VMEM),
        cost_estimate=pl.CostEstimate(flops=0, bytes_accessed=pieces[0].size * 10, transcendentals=0),
        name="pick",
    )(which[None].astype(jnp.int32), *pieces, *after)


def move(x, axis, step, size):
    return lax.ppermute(x, axis, [(i, (i + step) % size) for i in range(size)])


def swap_core(x):
    return move(x, "core", 1, 2)


def swap_outer(x):
    route = [(i, i + 1) for i in range(1, 15, 2)] + [(i + 1, i) for i in range(1, 15, 2)]
    return lax.ppermute(x, SKY, route)


def local(queries, key_states, value_states, key_blocks, global_block, w_out, grad_out):
    x, y, core = lax.axis_index("x_hi"), lax.axis_index("y"), lax.axis_index("core")
    side = lax.axis_index("x_lo")
    row = (x * 4 + y) * 2 + core
    root = global_block[0]
    ids = lax.dynamic_slice_in_dim(key_blocks, row, 1, 0)[0]
    above, below = ids[0], ids[1]
    inner_id = jnp.where(core == 0, below, above)
    outer_id = jnp.where(core == 0, above, below)
    live = (root != row) & (root != above) & (root != below)
    which = jnp.where(root % 2 == core, core, core + 2)
    info = jnp.stack(
        [inner_id >= 0, outer_id >= 0, live, core, root == row, y, side, 1 - side, which]
    ).astype(jnp.int32)
    q, k, v, go = queries[0], key_states[0], value_states[0], grad_out[0]
    w = lax.dynamic_slice_in_dim(w_out, core * HALF, HALF, 1)
    near = lax.all_gather(w, "z", axis=0, tiled=True)
    go_mine = lax.dynamic_slice_in_dim(go, core * HALF, HALF, 1)
    go_core = swap_core(lax.dynamic_slice_in_dim(go, (1 - core) * HALF, HALF, 1))
    kv = jnp.stack([k, v])
    inner = swap_core(kv)
    outer = swap_outer(kv)
    far = move(w, "x_lo", 1, 2)

    root_y, root_x = (root // 2) % 4, root // 8
    pieces = pack(info, k, v, inner, (go_core,))
    arrived = [pieces[0]] + [move(pieces[r], "y", r, 4) for r in range(1, 4)]
    mine = pick((y - root_y) % 4, arrived, (outer,))
    far = lax.all_gather(hold(far, (mine,)), "z", axis=0, tiled=True)
    ga_own, ga_core = project(go_mine[None], go_core[None], (0, 0), near, (arrived[1],))
    other = move(mine, "x_hi", 1, 2)
    quarter = pick((root_x - x) % 2, (mine, other), (ga_own,))
    ga_near = (ga_own, swap_core(ga_core))
    held = [quarter] + [move(quarter, "y", -r, 4) for r in range(1, 4)]
    held[2] = hold(held[2], ga_near)
    rows = (q, k, v, inner, outer, *held, *[swap_core(h) for h in held])

    out = attention(0, 0, CHUNK, info, rows, ga_near, (), ())
    att, gq, own0, tin0, tout0, keep, send = out
    ga_own, ga_core = project(go_mine[None], go_core[None], (0, 0), far, tuple(held))
    ga_far = (ga_own, swap_core(ga_core))
    rin0, rout0 = swap_core(tin0), swap_outer(tout0)
    both0 = add(keep, swap_core(send))
    quarter0 = lax.psum_scatter(both0, "y", scatter_dimension=0, tiled=True)

    out = attention(1, 0, CHUNK, info, rows, ga_far, (att, gq), (both0,))
    att, gq, own1, tin1, tout1, keep, send = out
    rin1, rout1 = swap_core(tin1), swap_outer(tout1)
    both1 = split(keep, swap_core(send), (rin0, rout0))
    quarters = gather(quarter0, both1, (rin1, rout1))
    halves = add(quarters, move(quarters, "x_hi", 1, 2))
    grads = combine(0, info, own0, rin0, rout0, (), (quarters,))
    grads = combine(1, info, own1, rin1, rout1, grads, (halves,))
    sums = [halves] + [move(halves, "y", -r, 4) for r in range(1, 4)]
    sums[2] = hold(sums[2], grads)
    gk, gv = finish(info, sums, [swap_core(s) for s in sums], *grads)
    return tuple(a[None] for a in (att, gq, gk, gv))


def solution(mesh):
    inside = Mesh(mesh.devices.reshape(2, 4, 2, 4, 2), DP + SKY)
    rows = P(DP, SKY, None)
    return jax.shard_map(
        local,
        mesh=inside,
        in_specs=(rows, rows, rows, P(), P(), P(DP, None), rows),
        out_specs=(rows, rows, rows, rows),
        check_vma=False,
    )
```

```python
import functools
import math

import jax
import jax.numpy as jnp
from jax import lax
from jax.experimental import pallas as pl
from jax.experimental.pallas import tpu as pltpu
from jax.sharding import Mesh, PartitionSpec as P

HEADS = 24
HD = 128
BLK = 256
D = 3072
HALF = D // 2
PART = BLK // 4
ROWS = D // 8
PAIR = 2
SCALE = 1.0 / math.sqrt(HD)
LOG2E = 1.4426950408889634
DP = ("x_lo", "z")
SKY = ("x_hi", "y", "core")
CHUNK = 12
ACROSS = (((1,), (1,)), ((), ()))
F32 = jnp.float32
BF16 = jnp.bfloat16
VMEM = 60 * 2**20


ANY = pl.BlockSpec(memory_space=pl.ANY)


def project_kernel(mine_ref, theirs_ref, piece_ref, *rest):
    own_ref, send_ref = rest[-2:]
    piece = piece_ref[...]
    own_ref[...] = lax.dot_general(mine_ref[...], piece, ACROSS, preferred_element_type=F32)
    send_ref[...] = lax.dot_general(theirs_ref[...], piece, ACROSS, preferred_element_type=F32).astype(BF16)


def project(mine, theirs, places, w, after):
    width = w.shape[0]
    first = pl.BlockSpec((None, BLK, HALF), lambda p: (places[0], 0, 0))
    second = pl.BlockSpec((None, BLK, HALF), lambda p: (places[1], 0, 0))
    out = pl.BlockSpec((BLK, ROWS), lambda p: (0, p))
    return pl.pallas_call(
        project_kernel,
        grid=(width // ROWS,),
        in_specs=[first, second, pl.BlockSpec((ROWS, HALF), lambda p: (p, 0))] + [ANY] * len(after),
        out_specs=[out, out],
        out_shape=[jax.ShapeDtypeStruct((BLK, width), F32), jax.ShapeDtypeStruct((BLK, width), BF16)],
        compiler_params=pltpu.CompilerParams(vmem_limit_bytes=VMEM),
        cost_estimate=pl.CostEstimate(
            flops=4 * BLK * width * HALF, bytes_accessed=width * HALF * 2 + BLK * width * 6, transcendentals=0
        ),
        name="project",
    )(mine, theirs, w, *after)


def one_head(info, q, keys, values, ga):
    ga_r = ga.astype(F32).T
    ga_t = ga_r.astype(BF16)
    raw = [lax.dot_general(k, q, ACROSS, preferred_element_type=F32) for k in keys]
    yield
    grad_weights = [jnp.dot(v, ga_t, preferred_element_type=F32) for v in values]
    scores = []
    for j in range(4):
        s = raw[j] * (SCALE * LOG2E)
        if j > 0:
            s = s + jnp.where(info[j - 1] > 0, 0.0, -jnp.inf).astype(F32)
        scores.append(s)
    top = functools.reduce(jnp.maximum, [jnp.max(s, axis=0, keepdims=True) for s in scores])
    exps = [jnp.exp2(s - top) for s in scores]
    total = functools.reduce(jnp.add, [jnp.sum(e, axis=0, keepdims=True) for e in exps])
    inverse = 1.0 / total
    weights = [e * inverse for e in exps]
    weights_b = [p.astype(BF16) for p in weights]
    yield
    att_t = jnp.zeros((HD, BLK), F32)
    for j in range(4):
        att_t += jnp.dot(values[j].T, weights_b[j], preferred_element_type=F32)
    att_r = att_t.astype(BF16).astype(F32)
    attended = att_r.T.astype(BF16)
    delta = jnp.sum(ga_r * att_r, axis=0, keepdims=True)
    value_terms = [jnp.dot(p, ga, preferred_element_type=F32).astype(BF16) for p in weights_b]
    yield
    gq_t = jnp.zeros((HD, BLK), F32)
    key_terms = []
    for j in range(4):
        gs = (weights[j] * (grad_weights[j] - delta)).astype(BF16)
        gq_t += jnp.dot(keys[j].T, gs, preferred_element_type=F32)
        key_terms.append((jnp.dot(gs, q, preferred_element_type=F32) * SCALE).astype(BF16))
    yield attended, (gq_t * SCALE).T.astype(BF16), key_terms, value_terms


def attention_kernel(
    terms, rolled, info, q_ref, ko_ref, vo_ref, inner_ref, outer_ref, *rest
):
    parts, ga_refs = rest[:8], rest[8 : 8 + terms]
    att_ref, gq_ref, own_ref, tin_ref, tout_ref, keep_ref, send_ref = rest[-7:]
    core, y = info[3], info[5]
    heads = []
    for a in range(PAIR):
        c = slice(a * HD, (a + 1) * HD)
        ga = functools.reduce(jnp.add, [ref[:, c].astype(F32) for ref in ga_refs]).astype(BF16)
        held = jnp.concatenate([ref[:, c] for ref in parts[:4]], axis=0)
        theirs = jnp.concatenate([ref[:, c] for ref in parts[4:]], axis=0)
        keys = [ko_ref[:, c], inner_ref[0, :, c], outer_ref[0, :, c], jnp.where(core == 0, held, theirs)]
        values = [vo_ref[:, c], inner_ref[1, :, c], outer_ref[1, :, c], jnp.where(core == 0, theirs, held)]
        heads.append(one_head(info, q_ref[:, c], keys, values, ga))
    for _ in range(3):
        for h in heads:
            next(h)
    for a in range(PAIR):
        c = slice(a * HD, (a + 1) * HD)
        attended, grad_query, key_terms, value_terms = next(heads[a])
        att_ref[:, c] = attended
        gq_ref[:, c] = grad_query
        for ref, j in ((own_ref, 0), (tin_ref, 1), (tout_ref, 2)):
            ref[0, :, c] = key_terms[j]
            ref[1, :, c] = value_terms[j]
        keep = jnp.where(core == 0, key_terms[3], value_terms[3])
        send = jnp.where(core == 0, value_terms[3], key_terms[3])
        for r in range(4):
            place = pl.multiple_of(lax.rem(y + r, 4) * PART, PART) if rolled else r * PART
            keep_ref[pl.ds(place, PART), c] = keep[r * PART : (r + 1) * PART]
            send_ref[pl.ds(place, PART), c] = send[r * PART : (r + 1) * PART]


def attention(part, begin, count, info, rows, ga, prior, after):
    wide = PAIR * HD
    whole = CHUNK // PAIR
    steps = count // PAIR
    first = begin // PAIR

    def head(t, info):
        return (0, info[6 + part] * whole + first + t)

    def heads(t, info):
        return (0, 0, info[6 + part] * whole + first + t)

    def col(t, *_):
        return (0, first + t)

    def pair(t, *_):
        return (0, 0, first + t)

    one = (BLK, wide)
    two = (2, BLK, wide)
    in_specs = (
        [pl.BlockSpec(one, head)] * 3
        + [pl.BlockSpec(two, heads)] * 2
        + [pl.BlockSpec((PART, wide), head)] * 8
        + [pl.BlockSpec(one, col)] * len(ga)
        + [ANY] * (len(prior) + len(after))
    )
    out_specs = (
        [pl.BlockSpec(one, head)] * 2 + [pl.BlockSpec(two, pair)] * 3 + [pl.BlockSpec(one, col)] * 2
    )
    full = jax.ShapeDtypeStruct((BLK, D), BF16)
    stacked = jax.ShapeDtypeStruct((2, BLK, CHUNK * HD), BF16)
    single = jax.ShapeDtypeStruct((BLK, CHUNK * HD), BF16)
    return pl.pallas_call(
        functools.partial(attention_kernel, len(ga), False),
        grid_spec=pltpu.PrefetchScalarGridSpec(
            num_scalar_prefetch=1, grid=(steps,), in_specs=in_specs, out_specs=out_specs
        ),
        out_shape=[full, full, stacked, stacked, stacked, single, single],
        input_output_aliases={14 + len(ga) + i: i for i in range(len(prior))},
        compiler_params=pltpu.CompilerParams(vmem_limit_bytes=VMEM),
        cost_estimate=pl.CostEstimate(
            flops=count * 12 * BLK * 4 * BLK * HD,
            bytes_accessed=count * BLK * HD * 2 * 21,
            transcendentals=count * BLK * 4 * BLK,
        ),
        name="attention",
    )(info, *rows, *ga, *prior, *after)


def combine_kernel(info, own_ref, rin_ref, rout_ref, *rest):
    gk_ref, gv_ref = rest[-2:]
    total = own_ref[...].astype(F32) + rin_ref[...].astype(F32) + rout_ref[...].astype(F32)
    gk_ref[...] = total[0].astype(BF16)
    gv_ref[...] = total[1].astype(BF16)


def combine(part, info, own, rin, rout, prior, after):
    wide = 4 * HD
    steps = CHUNK * HD // wide
    two = pl.BlockSpec((2, BLK, wide), lambda t, *_: (0, 0, t))
    full = jax.ShapeDtypeStruct((BLK, D), BF16)
    return pl.pallas_call(
        combine_kernel,
        grid_spec=pltpu.PrefetchScalarGridSpec(
            num_scalar_prefetch=1,
            grid=(steps,),
            in_specs=[two, two, two] + [ANY] * (len(prior) + len(after)),
            out_specs=[pl.BlockSpec((BLK, wide), lambda t, info: (0, info[6 + part] * steps + t))] * 2,
        ),
        out_shape=[full, full],
        input_output_aliases={4: 0, 5: 1} if prior else {},
        compiler_params=pltpu.CompilerParams(vmem_limit_bytes=VMEM),
        cost_estimate=pl.CostEstimate(
            flops=CHUNK * BLK * HD * 4, bytes_accessed=CHUNK * BLK * HD * 2 * 8, transcendentals=0
        ),
        name="combine",
    )(info, own, rin, rout, *prior, *after)


def finish_kernel(info, *refs):
    gk_ref, gv_ref, ok_ref, ov_ref = refs[8:]
    core, hit, y = info[3], info[4], info[5]
    ok_ref[...] = gk_ref[...]
    ov_ref[...] = gv_ref[...]

    @pl.when(hit > 0)
    def _():
        for r in range(4):
            rows = pl.ds(pl.multiple_of(lax.rem(y + r, 4) * PART, PART), PART)
            mine, theirs = refs[r][...].astype(F32), refs[4 + r][...].astype(F32)
            k_sum, v_sum = jnp.where(core == 0, mine, theirs), jnp.where(core == 0, theirs, mine)
            ok_ref[rows] = (gk_ref[rows].astype(F32) + k_sum).astype(BF16)
            ov_ref[rows] = (gv_ref[rows].astype(F32) + v_sum).astype(BF16)


def finish(info, mine, theirs, gk, gv):
    wide = 4 * HD
    steps = CHUNK * HD // wide

    def head(t, info):
        return (0, lax.rem(info[6] * steps + t, 2 * steps))

    here = pl.BlockSpec((BLK, wide), head)
    sums = pl.BlockSpec((PART, wide), lambda t, *_: (0, t))
    full = jax.ShapeDtypeStruct((BLK, D), BF16)
    return pl.pallas_call(
        finish_kernel,
        grid_spec=pltpu.PrefetchScalarGridSpec(
            num_scalar_prefetch=1, grid=(2 * steps,), in_specs=[sums] * 8 + [here, here], out_specs=[here, here]
        ),
        out_shape=[full, full],
        input_output_aliases={9: 0, 10: 1},
        compiler_params=pltpu.CompilerParams(vmem_limit_bytes=VMEM),
        cost_estimate=pl.CostEstimate(flops=BLK * D * 2, bytes_accessed=BLK * D * 12, transcendentals=0),
        name="finish",
    )(info, *mine, *theirs, gk, gv)


def add_kernel(a_ref, b_ref, *rest):
    rest[-1][...] = (a_ref[...].astype(F32) + b_ref[...].astype(F32)).astype(BF16)


def add(a, b, after=()):
    width = a.shape[1] // 2
    spec = pl.BlockSpec((a.shape[0], width), lambda t: (0, t))
    return pl.pallas_call(
        add_kernel,
        grid=(2,),
        in_specs=[spec, spec] + [ANY] * len(after),
        out_specs=spec,
        out_shape=jax.ShapeDtypeStruct(a.shape, BF16),
        compiler_params=pltpu.CompilerParams(vmem_limit_bytes=VMEM),
        cost_estimate=pl.CostEstimate(flops=a.size, bytes_accessed=a.size * 6, transcendentals=0),
        name="add",
    )(a, b, *after)


def split_kernel(a_ref, b_ref, *rest):
    for r in range(4):
        rows = slice(r * PART, (r + 1) * PART)
        rest[-4 + r][...] = (a_ref[rows].astype(F32) + b_ref[rows].astype(F32)).astype(BF16)


def split(a, b, after):
    width = a.shape[1] // 2
    spec = pl.BlockSpec((BLK, width), lambda t: (0, t))
    return pl.pallas_call(
        split_kernel,
        grid=(2,),
        in_specs=[spec, spec] + [ANY] * len(after),
        out_specs=[pl.BlockSpec((PART, width), lambda t: (0, t))] * 4,
        out_shape=[jax.ShapeDtypeStruct((PART, a.shape[1]), BF16)] * 4,
        compiler_params=pltpu.CompilerParams(vmem_limit_bytes=VMEM),
        cost_estimate=pl.CostEstimate(flops=a.size, bytes_accessed=a.size * 6, transcendentals=0),
        name="split",
    )(a, b, *after)


def gather_kernel(*refs):
    half = refs[-1].shape[1] // 2
    for part in range(2):
        total = functools.reduce(jnp.add, [ref[...].astype(F32) for ref in refs[4 * part : 4 * part + 4]])
        refs[-1][:, part * half : (part + 1) * half] = total.astype(BF16)


def arrive(pieces):
    return [pieces[0]] + [move(pieces[r], "y", r, 4) for r in range(1, 4)]


def gather(first, second, after):
    whole = pl.BlockSpec(memory_space=pltpu.VMEM)
    return pl.pallas_call(
        gather_kernel,
        in_specs=[whole] * 8 + [ANY] * len(after),
        out_specs=whole,
        out_shape=jax.ShapeDtypeStruct((PART, D), BF16),
        compiler_params=pltpu.CompilerParams(vmem_limit_bytes=VMEM),
        cost_estimate=pl.CostEstimate(flops=PART * D * 4, bytes_accessed=PART * D * 10, transcendentals=0),
        name="gather",
    )(*first, *second, *after)


def hold_kernel(*refs):
    del refs


def hold(x, after):
    return pl.pallas_call(
        hold_kernel,
        in_specs=[ANY] * (1 + len(after)),
        out_specs=ANY,
        out_shape=jax.ShapeDtypeStruct(x.shape, x.dtype),
        input_output_aliases={0: 0},
        cost_estimate=pl.CostEstimate(flops=0, bytes_accessed=0, transcendentals=0),
        name="hold",
    )(x, *after)


def pack_kernel(info, k_ref, v_ref, inner_ref, *outs):
    outs = outs[-4:]
    y, which = info[5], info[8]
    for r in range(4):
        rows = pl.ds(pl.multiple_of(lax.rem(y + r, 4) * PART, PART), PART)
        for i in range(4):

            @pl.when(which == i)
            def _():
                outs[r][...] = (k_ref, v_ref, inner_ref.at[0], inner_ref.at[1])[i][rows]


def pack(info, k, v, inner, after):
    def col(t, *_):
        return (0, t)

    wide = D // 2
    return pl.pallas_call(
        pack_kernel,
        grid_spec=pltpu.PrefetchScalarGridSpec(
            num_scalar_prefetch=1,
            grid=(2,),
            in_specs=[pl.BlockSpec((BLK, wide), col)] * 2
            + [pl.BlockSpec((2, BLK, wide), lambda t, *_: (0, 0, t))]
            + [ANY] * len(after),
            out_specs=[pl.BlockSpec((PART, wide), col)] * 4,
        ),
        out_shape=[jax.ShapeDtypeStruct((PART, D), BF16)] * 4,
        compiler_params=pltpu.CompilerParams(vmem_limit_bytes=VMEM),
        cost_estimate=pl.CostEstimate(flops=0, bytes_accessed=BLK * D * 10, transcendentals=0),
        name="pack",
    )(info, k, v, inner, *after)


def pick(which, pieces, after=()):
    count = len(pieces)

    def kernel(which, *refs):
        for i in range(count):

            @pl.when(which[0] == i)
            def _():
                refs[-1][...] = refs[i][...]

    spec = pl.BlockSpec(pieces[0].shape, lambda t, *_: (0, 0))
    return pl.pallas_call(
        kernel,
        grid_spec=pltpu.PrefetchScalarGridSpec(
            num_scalar_prefetch=1, grid=(1,), in_specs=[spec] * count + [ANY] * len(after), out_specs=spec
        ),
        out_shape=jax.ShapeDtypeStruct(pieces[0].shape, BF16),
        compiler_params=pltpu.CompilerParams(vmem_limit_bytes=VMEM),
        cost_estimate=pl.CostEstimate(flops=0, bytes_accessed=pieces[0].size * 10, transcendentals=0),
        name="pick",
    )(which[None].astype(jnp.int32), *pieces, *after)


def move(x, axis, step, size):
    return lax.ppermute(x, axis, [(i, (i + step) % size) for i in range(size)])


def swap_core(x):
    return move(x, "core", 1, 2)


def swap_outer(x):
    route = [(i, i + 1) for i in range(1, 15, 2)] + [(i + 1, i) for i in range(1, 15, 2)]
    return lax.ppermute(x, SKY, route)


def local(queries, key_states, value_states, key_blocks, global_block, w_out, grad_out):
    x, y, core = lax.axis_index("x_hi"), lax.axis_index("y"), lax.axis_index("core")
    side = lax.axis_index("x_lo")
    row = (x * 4 + y) * 2 + core
    root = global_block[0]
    ids = lax.dynamic_slice_in_dim(key_blocks, row, 1, 0)[0]
    above, below = ids[0], ids[1]
    inner_id = jnp.where(core == 0, below, above)
    outer_id = jnp.where(core == 0, above, below)
    live = (root != row) & (root != above) & (root != below)
    which = jnp.where(root % 2 == core, core, core + 2)
    info = jnp.stack(
        [inner_id >= 0, outer_id >= 0, live, core, root == row, y, side, 1 - side, which]
    ).astype(jnp.int32)
    q, k, v, go = queries[0], key_states[0], value_states[0], grad_out[0]
    w = lax.dynamic_slice_in_dim(w_out, core * HALF, HALF, 1)
    near = lax.all_gather(w, "z", axis=0, tiled=True)
    go_mine = lax.dynamic_slice_in_dim(go, core * HALF, HALF, 1)
    go_core = swap_core(lax.dynamic_slice_in_dim(go, (1 - core) * HALF, HALF, 1))
    kv = jnp.stack([k, v])
    inner = swap_core(kv)
    outer = swap_outer(kv)
    far = move(w, "x_lo", 1, 2)

    root_y, root_x = (root // 2) % 4, root // 8
    pieces = pack(info, k, v, inner, (go_core,))
    arrived = [pieces[0]] + [move(pieces[r], "y", r, 4) for r in range(1, 4)]
    mine = pick((y - root_y) % 4, arrived, (outer,))
    far = lax.all_gather(hold(far, (mine,)), "z", axis=0, tiled=True)
    ga_own, ga_core = project(go_mine[None], go_core[None], (0, 0), near, (arrived[1],))
    other = move(mine, "x_hi", 1, 2)
    quarter = pick((root_x - x) % 2, (mine, other), (ga_own,))
    ga_near = (ga_own, swap_core(ga_core))
    held = [quarter] + [move(quarter, "y", -r, 4) for r in range(1, 4)]
    held[2] = hold(held[2], ga_near)
    rows = (q, k, v, inner, outer, *held, *[swap_core(h) for h in held])

    out = attention(0, 0, CHUNK, info, rows, ga_near, (), ())
    att, gq, own0, tin0, tout0, keep, send = out
    ga_own, ga_core = project(go_mine[None], go_core[None], (0, 0), far, tuple(held))
    ga_far = (ga_own, swap_core(ga_core))
    rin0, rout0 = swap_core(tin0), swap_outer(tout0)
    both0 = split(keep, swap_core(send), ())
    arrived0 = arrive(both0)

    out = attention(1, 0, CHUNK, info, rows, ga_far, (att, gq), tuple(both0))
    att, gq, own1, tin1, tout1, keep, send = out
    rin1, rout1 = swap_core(tin1), swap_outer(tout1)
    both1 = split(keep, swap_core(send), (rin0, rout0, *arrived0[1:]))
    quarters = gather(arrived0, arrive(both1), (rin1, rout1))
    halves = add(quarters, move(quarters, "x_hi", 1, 2))
    grads = combine(0, info, own0, rin0, rout0, (), (quarters,))
    grads = combine(1, info, own1, rin1, rout1, grads, (halves,))
    sums = [halves] + [move(halves, "y", -r, 4) for r in range(1, 4)]
    sums[2] = hold(sums[2], grads)
    gk, gv = finish(info, sums, [swap_core(s) for s in sums], *grads)
    return tuple(a[None] for a in (att, gq, gk, gv))


def solution(mesh):
    inside = Mesh(mesh.devices.reshape(2, 4, 2, 4, 2), DP + SKY)
    rows = P(DP, SKY, None)
    return jax.shard_map(
        local,
        mesh=inside,
        in_specs=(rows, rows, rows, P(), P(), P(DP, None), rows),
        out_specs=(rows, rows, rows, rows),
        check_vma=False,
    )
```
